256 devices in a mesh: wide: 8 (over x, core), narrow: 32 (over z, y).
Axes of the slice: x: 4, y: 4, z: 8, core: 2. Of those that a mesh axis runs over, the one named last changes fastest.
Arguments:
- rhs: float32 [65536, 2, 128], P(('wide', 'narrow')), may hold values from -6 to 6
- fine_face: float32 [65536, 2, 128], P(('wide', 'narrow')), may hold values from 0.2 to 2
- fine_sink: float32 [65536, 2, 128], P(('wide', 'narrow')), may hold values from 0.01 to 0.5
- fine_kap: float32 [65536, 128], P(('wide', 'narrow')), may hold values from -0.9 to 0.9
- cell_mask: int32 [65536, 128], P(('wide', 'narrow')), may hold values 0 or 1
- block_aggregate: int32 [65536], P(('wide', 'narrow')), may hold values from 0 to 2047, as said below
- coarse_face: float32 [16384, 2, 128], P(('wide', 'narrow')), may hold values from 0.2 to 2
- coarse_sink: float32 [16384, 2, 128], P(('wide', 'narrow')), may hold values from 0.02 to 1
- coarse_kap: float32 [16384, 128], P(('wide', 'narrow')), may hold values from -0.9 to 0.9
Outputs:
- solution: float32 [65536, 2, 128], P(('wide', 'narrow'))
The draws below stay inside these ranges and needn't reach their ends.
Inputs may be any that keep to these rules, and one draw needn't show every extreme that they name: `block_aggregate`: aggregates are numbered within the group of devices sharing a wide index; aggregate a lives on the device with narrow index a // 64; the 256 blocks of one device name aggregates of any one such owner at most 16 times, and in every group one owner is named exactly 16 times by the blocks of every device of the group.
All inputs are finite; a program needn't handle non-finite values. No bound on the sum of `cell_mask` on one device may be relied on, other than what follows from the above.
Results may differ from the reference program's by a relative error of at most 0.00005.
Values sent between devices are 32-bit elements; how exact they have to be, the bound alone decides.
No kernel may reach another device: no remote copies, remote signals or barrier semaphores. Data moves between devices by JAX's collectives and lax.ppermute only.
A program may use at most 192 MiB of HBM per device.

```python
import math
import jax
import jax.numpy as jnp

CELLS = 128
BLK_DEV = 256
AGG_DEV = 64
PRE = 2
POST = 2
CSWEEPS = 4
LEVELS = 4
BLOCKS = 65536
AGGS = 16384
N_WIDE = 8
N_NARROW = 32


def draw_block_aggregate(key, part):
    key = jax.random.fold_in(key, 11)
    route_cap = max(2, 2 * BLK_DEV // N_NARROW)
    slot_total_count = N_NARROW * route_cap
    preferred_owner = jax.random.randint(jax.random.fold_in(key, 1), (N_WIDE,), 0, N_NARROW)

    def one_device(processor_index):
        inner = jax.random.fold_in(key, 100 + processor_index)
        rank_order = jax.random.permutation(jax.random.fold_in(inner, 0), slot_total_count)
        slot_holder_rank = jnp.arange(slot_total_count, dtype=jnp.int32) // route_cap
        extra_credit = jnp.where(slot_holder_rank == preferred_owner[processor_index // N_NARROW], slot_total_count, 0)
        score_table = rank_order.astype(jnp.int32) + extra_credit.astype(jnp.int32)
        chosen = jnp.argsort(-score_table)[:BLK_DEV]
        owners = slot_holder_rank[chosen]
        mixing = jax.random.permutation(jax.random.fold_in(inner, 1), BLK_DEV)
        owners = owners[mixing]
        within = jax.random.randint(jax.random.fold_in(inner, 2), (BLK_DEV,), 0, AGG_DEV)
        return (owners * AGG_DEV + within).astype(jnp.int32)
    devices = jnp.arange(N_WIDE * N_NARROW, dtype=jnp.int32)
    return jax.vmap(one_device)(devices).reshape(-1)


def with_ends(array, own_key, smallest, top_value):
    shape = array.shape
    place = [jax.random.randint(jax.random.fold_in(own_key, axis), (), 0, shape[axis]) for axis in range(len(shape))]
    array = array.at[tuple(place)].set(smallest)
    longest = shape.index(max(shape))
    place[longest] = (place[longest] + 1) % shape[longest]
    return array.at[tuple(place)].set(top_value)


def level_of(stream_key, shape, split, low, high):
    def one(axis_at, blocks):
        steps = jax.random.uniform(jax.random.fold_in(jax.random.fold_in(stream_key, 6), axis_at), (blocks,), jnp.float32, low / len(split), high / len(split))
        return jnp.repeat(jnp.exp(steps), shape[axis_at] // blocks).reshape((-1,) + (1,) * (len(shape) - axis_at - 1))

    level = one(*split[0])
    for cut in split[1:]:
        level = level * one(*cut)
    return level


def normal_values(key, dims, spread, bound, pieces=(), kind=jnp.bfloat16):
    array = spread * jax.random.normal(key, dims, jnp.float32)
    if pieces:
        array = array * level_of(key, dims, pieces, -0.22, 0.18)
    return jnp.clip(array, -bound, bound).astype(kind)


def setup_inputs(seed: int = 0) -> dict:
    keys = jax.random.split(jax.random.key(seed), 10)
    rhs = normal_values(keys[0], (BLOCKS, 2, CELLS), 1.0, 6.0, ((0, 256),), jnp.float32)
    fine_face = jnp.clip(jnp.exp(math.log(2.0) - 2.3025851 * jax.random.uniform(keys[1], (BLOCKS, 2, CELLS), jnp.float32) ** level_of(keys[1], (BLOCKS, 2, CELLS), ((0, 256),), -0.2, 0.2)), 0.2, 2.0)
    fine_sink = jnp.clip(jnp.exp(math.log(0.5) - 3.912023 * jax.random.uniform(keys[2], (BLOCKS, 2, CELLS), jnp.float32) ** level_of(keys[2], (BLOCKS, 2, CELLS), ((0, 256),), -0.2, 0.2)), 0.01, 0.5)
    fine_kap = jnp.clip(jax.random.uniform(keys[3], (BLOCKS, CELLS), jnp.float32, -0.9, 0.9) * level_of(keys[3], (BLOCKS, CELLS), ((0, 256),), -0.4, 0.0), -0.9, 0.9)
    cell_mask = with_ends((jax.random.randint(keys[4], (BLOCKS, CELLS), 0, 8) < 7).astype(jnp.int32), jax.random.fold_in(keys[4], 1), 0, 1)
    block_aggregate = draw_block_aggregate(jax.random.fold_in(keys[9], 71), 0)
    coarse_face = jnp.clip(jnp.exp(math.log(2.0) - 2.3025851 * jax.random.uniform(keys[6], (AGGS, 2, CELLS), jnp.float32) ** level_of(keys[6], (AGGS, 2, CELLS), ((0, 256),), -0.2, 0.2)), 0.2, 2.0)
    coarse_sink = jnp.clip(jnp.exp(math.log(1.0) - 3.912023 * jax.random.uniform(keys[7], (AGGS, 2, CELLS), jnp.float32) ** level_of(keys[7], (AGGS, 2, CELLS), ((0, 256),), -0.2, 0.2)), 0.02, 1.0)
    coarse_kap = jnp.clip(jax.random.uniform(keys[8], (AGGS, CELLS), jnp.float32, -0.9, 0.9) * level_of(keys[8], (AGGS, CELLS), ((0, 256),), -0.4, 0.0), -0.9, 0.9)
    return dict(rhs=rhs, fine_face=fine_face, fine_sink=fine_sink, fine_kap=fine_kap, cell_mask=cell_mask, block_aggregate=block_aggregate, coarse_face=coarse_face, coarse_sink=coarse_sink, coarse_kap=coarse_kap)


OMEGA = 0.8

def prev_cells(field, before):
    lastcol = field[..., -1]
    carried = jnp.concatenate([before[None], lastcol[:-1]], axis=0)
    return jnp.concatenate([carried[..., None], field[..., :-1]], axis=-1)

def next_cells(field, after):
    firstcol = field[..., 0]
    carried = jnp.concatenate([firstcol[1:], after[None]], axis=0)
    return jnp.concatenate([field[..., 1:], carried[..., None]], axis=-1)

def operate(field, behind, ahead, faces, faces_left, diagonal, coupling):
    crossed = jnp.stack([field[:, 1], field[:, 0]], axis=1)
    return diagonal * field - faces_left * behind - faces * ahead - coupling[:, None, :] * crossed

def inverse_parts(diagonal, coupling):
    determinant = diagonal[:, 0] * diagonal[:, 1] - coupling * coupling
    return (diagonal[:, 1] / determinant, diagonal[:, 0] / determinant, coupling / determinant)

def relax(field, misfit, inverse):
    first_part = inverse[0] * misfit[:, 0] + inverse[2] * misfit[:, 1]
    second_part = inverse[2] * misfit[:, 0] + inverse[1] * misfit[:, 1]
    return field + OMEGA * jnp.stack([first_part, second_part], axis=1)

def closed_apply(field, data):
    edge = jnp.zeros(field.shape[1:-1], jnp.float32)
    return operate(field, prev_cells(field, edge), next_cells(field, edge), data[0], data[1], data[2], data[3])

def level_setup(faces, sinks, coupling):
    faces_left = prev_cells(faces, jnp.zeros(faces.shape[1:-1], jnp.float32))
    diagonal = sinks + faces_left + faces
    return (faces, faces_left, diagonal, coupling, inverse_parts(diagonal, coupling))

def fine_setup(face, sink, kap, live):
    live_next = next_cells(live, jnp.zeros((), jnp.float32))
    faces = face * live[:, None, :] * live_next[:, None, :]
    faces_left = prev_cells(faces, jnp.zeros((2,), jnp.float32))
    diagonal = sink + faces_left + faces
    coupling = kap * jnp.sqrt(sink[:, 0] * sink[:, 1]) * live
    return (faces, faces_left, diagonal, coupling, inverse_parts(diagonal, coupling))

def smooth(field, source, data, sweeps):
    for _ in range(sweeps):
        field = relax(field, source - closed_apply(field, data), data[4])
    return field

def start_smooth(source, data, sweeps):
    field = relax(jnp.zeros_like(source), source, data[4])
    return smooth(field, source, data, sweeps - 1)

def fold(values, level):
    width = 2 ** level
    shape = values.shape
    paired = values.reshape((N_WIDE // (2 * width), 2, width) + shape[1:])
    total = paired[:, 0] + paired[:, 1]
    return jnp.stack([total, total], axis=1).reshape(shape)

def reference(rhs, fine_face, fine_sink, fine_kap, cell_mask, block_aggregate, coarse_face, coarse_sink, coarse_kap):
    rows = N_NARROW * BLK_DEV
    group_aggs = N_NARROW * AGG_DEV

    def grouped(values):
        return values.reshape((N_WIDE, rows) + values.shape[1:])
    live = grouped(cell_mask).astype(jnp.float32)
    fine_data = jax.vmap(fine_setup)(grouped(fine_face), grouped(fine_sink), grouped(fine_kap), live)
    source = grouped(rhs) * live[:, :, None, :]
    field = jax.vmap(lambda src, dat: start_smooth(src, dat, PRE))(source, fine_data)
    misfit = source - jax.vmap(closed_apply)(field, fine_data)
    aggregate = grouped(block_aggregate)
    offsets = jnp.arange(N_WIDE, dtype=jnp.int32) * group_aggs
    identity = (aggregate + offsets[:, None]).reshape(-1)
    restricted = jax.ops.segment_sum(misfit.reshape((-1, 2, CELLS)), identity, num_segments=N_WIDE * group_aggs)
    source_c = restricted.reshape((N_WIDE, group_aggs, 2, CELLS))
    faces_c = coarse_face.reshape((N_WIDE, N_NARROW, AGG_DEV, 2, CELLS)).at[:, :, -1, :, -1].set(0.0)
    faces_c = faces_c.reshape((N_WIDE, group_aggs, 2, CELLS))
    sinks_c = coarse_sink.reshape((N_WIDE, group_aggs, 2, CELLS))
    kaps_c = coarse_kap.reshape((N_WIDE, group_aggs, CELLS))
    coupling_c = kaps_c * jnp.sqrt(sinks_c[:, :, 0] * sinks_c[:, :, 1])
    saved = []
    correction = source_c
    for level in range(LEVELS):
        data = jax.vmap(level_setup)(faces_c, sinks_c, coupling_c)
        if level < LEVELS - 1:
            correction = jax.vmap(lambda src, dat: start_smooth(src, dat, PRE))(source_c, data)
            leftover = source_c - jax.vmap(closed_apply)(correction, data)
            saved.append((correction, source_c, data))
            source_c = fold(leftover, level)
            faces_c = fold(faces_c, level)
            sinks_c = fold(sinks_c, level)
            coupling_c = fold(coupling_c, level)
        else:
            correction = jax.vmap(lambda src, dat: start_smooth(src, dat, CSWEEPS))(source_c, data)
    for level in reversed(range(LEVELS - 1)):
        below, level_source, data = saved[level]
        correction = jax.vmap(lambda fld, src, dat: smooth(fld, src, dat, POST))(below + correction, level_source, data)
    lifted = jax.vmap(lambda values, index: values[index])(correction, aggregate)
    field = field + lifted
    field = jax.vmap(lambda fld, src, dat: smooth(fld, src, dat, POST))(field, source, fine_data)
    return field.reshape((N_WIDE * rows, 2, CELLS))
```

```python
import jax
import jax.numpy as jnp
from jax import lax
from jax.experimental import pallas as pl
from jax.experimental.pallas import tpu as pltpu
from jax.sharding import PartitionSpec as P

OMEGA = 0.8
LANES = 128
BLK = 256
AGG = 64
NARROW = 32
CAP = 16
UNIT = 2 * (CAP + 1)
F32, BF16, I32 = jnp.float32, jnp.bfloat16, jnp.int32


def iota(shape, dim):
    return lax.broadcasted_iota(I32, shape, dim)


def chain_next(v):
    ahead = pltpu.roll(v, LANES - 1, 1)
    below = pltpu.roll(ahead, v.shape[0] - 1, 0)
    return jnp.where(iota(v.shape, 1) == LANES - 1, below, ahead)


def chain_prev(v):
    behind = pltpu.roll(v, 1, 1)
    above = pltpu.roll(behind, 1, 0)
    return jnp.where(iota(v.shape, 1) == 0, above, behind)


def row_next(v):
    return pltpu.roll(v, LANES - 1, 1)


def row_prev(v):
    return pltpu.roll(v, 1, 1)


class Level:
    def __init__(self, faces, sinks, coupling, prev, nxt):
        self.prev, self.nxt = prev, nxt
        self.faces = faces
        self.left = [prev(f) for f in faces]
        self.diag = [s + l + f for s, l, f in zip(sinks, self.left, faces)]
        self.coupling = coupling
        scale = OMEGA / (self.diag[0] * self.diag[1] - coupling * coupling)
        self.inv = (self.diag[1] * scale, self.diag[0] * scale, coupling * scale)

    def misfit(self, v, source):
        return [
            source[f]
            - (
                self.diag[f] * v[f]
                - self.left[f] * self.prev(v[f])
                - self.faces[f] * self.nxt(v[f])
                - self.coupling * v[1 - f]
            )
            for f in (0, 1)
        ]

    def step(self, r):
        return [
            self.inv[0] * r[0] + self.inv[2] * r[1],
            self.inv[2] * r[0] + self.inv[1] * r[1],
        ]

    def smooth(self, v, source, sweeps):
        for _ in range(sweeps):
            d = self.step(self.misfit(v, source))
            v = [v[0] + d[0], v[1] + d[1]]
        return v

    def start(self, source, sweeps):
        return self.smooth(self.step(source), source, sweeps - 1)


def fine_level(face, sink, kap, live, prev, nxt, last):
    live_next = jnp.where(last, 0.0, nxt(live))
    both = live * live_next
    faces = [f * both for f in face]
    coupling = kap * jnp.sqrt(sink[0] * sink[1]) * live
    return Level(faces, sink, coupling, prev, nxt)


def last_cell(shape):
    return (iota(shape, 0) == shape[0] - 1) & (iota(shape, 1) == LANES - 1)


def split3(x):
    hi = x.astype(BF16)
    rest = x - hi.astype(F32)
    mid = rest.astype(BF16)
    return hi, mid, (rest - mid.astype(F32)).astype(BF16)


def select_rows(onehot, x):
    total = None
    for part in split3(x):
        term = jnp.dot(onehot, part, preferred_element_type=F32)
        total = term if total is None else total + term
    return total


def as_bf16(mask):
    return jnp.where(mask, 1.0, 0.0).astype(BF16)


def planar(ref, rows):
    return [ref[pl.ds(f, rows, stride=2), :] for f in (0, 1)]


def fine_inputs(rhs, face, sink, kap, mask):
    live = mask[...].astype(F32)
    shape = (BLK, LANES)
    data = fine_level(
        planar(face, BLK), planar(sink, BLK), kap[...], live, chain_prev, chain_next, last_cell(shape)
    )
    source = [r * live for r in planar(rhs, BLK)]
    return data, source


def pre_kernel(narrow, rhs, face, sink, kap, mask, agg, out, slots):
    n = narrow[0]
    data, source = fine_inputs(rhs, face, sink, kap, mask)
    field = data.start(source, 2)
    misfit = data.misfit(field, source)
    row, lane = iota((BLK, LANES), 0), iota((BLK, LANES), 1)
    drop = ((row == BLK - 1) & (lane >= LANES - 3) & (n < NARROW - 1)) | (
        (row == 0) & (lane < 3) & (n > 0)
    )
    misfit = jnp.concatenate([jnp.where(drop, 0.0, m) for m in misfit], axis=1)

    label = agg[...]
    owner = label // AGG
    within = label - owner * AGG
    owned = iota((NARROW, BLK), 0) == owner
    before = as_bf16(iota((BLK, BLK), 0) < iota((BLK, BLK), 1))
    counts = jnp.dot(as_bf16(owned), before, preferred_element_type=F32)
    rank = jnp.sum(jnp.where(owned, counts, 0.0), axis=0, keepdims=True).astype(I32)
    slot = owner * CAP + rank
    put = as_bf16(iota((NARROW * CAP, BLK), 0) == slot)
    rows = select_rows(put, misfit)
    for o in range(NARROW):
        for f in (0, 1):
            out[pl.ds(o * UNIT + f, CAP, stride=2), :] = rows[
                o * CAP : (o + 1) * CAP, f * LANES : (f + 1) * LANES
            ]

    block = iota((1, BLK), 1)
    code = within + 1 + jnp.where(block == 0, 64, 0) + jnp.where(block == BLK - 1, 128, 0)
    coded = jnp.where(owned, code.astype(F32), 0.0).astype(BF16)
    at_rank = as_bf16(iota((LANES, BLK), 0) % CAP == rank)
    labels = lax.dot_general(
        coded, at_rank, (((1,), (1,)), ((), ())), preferred_element_type=F32
    )
    out[pl.ds(2 * CAP, NARROW, stride=UNIT), :] = labels

    lane1 = iota((1, LANES), 1)
    edges = jnp.zeros((1, LANES), F32)
    quantities = [(ref, 2, f) for ref in (rhs, face, sink) for f in (0, 1)]
    quantities += [(kap, 1, 0), (mask, 1, 0)]
    for q, (ref, stride, f) in enumerate(quantities):
        final = (BLK - 1) * stride + f
        cells = jnp.where(
            lane1 >= LANES // 2, ref[final : final + 1, :], ref[f : f + 1, :]
        ).astype(F32)
        moved = pltpu.roll(cells, (16 * q + 8) % LANES, 1)
        edges = jnp.where(lane1 // 16 == q, moved, edges)
    out[pl.ds(2 * CAP + 1, NARROW, stride=UNIT), :] = jnp.broadcast_to(edges, (NARROW, LANES))

    slots[...] = jnp.transpose(jnp.broadcast_to(slot.astype(F32), (LANES, BLK)), (1, 0))


def interface_level(cells):
    lane = iota(cells.shape, 1)

    def quantity(q, fill):
        moved = cells if q == 0 else pltpu.roll(cells, LANES - 16 * q, 1)
        return jnp.where(lane < 16, moved, fill)

    rhs = [quantity(0, 0.0), quantity(1, 0.0)]
    face = [quantity(2, 0.0), quantity(3, 0.0)]
    sink = [quantity(4, 1.0), quantity(5, 1.0)]
    kap, live = quantity(6, 0.0), quantity(7, 0.0)
    data = fine_level(face, sink, kap, live, row_prev, row_next, lane == LANES - 1)
    source = [r * live for r in rhs]
    return data, source


def coarse_level(ref):
    part = [ref[k * AGG : (k + 1) * AGG, :] for k in range(5)]
    return Level(part[0:2], part[2:4], part[4], chain_prev, chain_next)


def store2(ref, v):
    ref[0:AGG, :] = v[0]
    ref[AGG : 2 * AGG, :] = v[1]


def load2(ref):
    return [ref[0:AGG, :], ref[AGG : 2 * AGG, :]]


def coef_kernel(face, sink, kap, out):
    faces, sinks = planar(face, AGG), planar(sink, AGG)
    last = last_cell((AGG, LANES))
    for f in (0, 1):
        out[f * AGG : (f + 1) * AGG, :] = jnp.where(last, 0.0, faces[f])
        out[(2 + f) * AGG : (3 + f) * AGG, :] = sinks[f]
    out[4 * AGG : 5 * AGG, :] = kap[...] * jnp.sqrt(sinks[0] * sinks[1])


def restrict_kernel(narrow, recv, coef, leftover, below, source_out, marks, own_edges):
    n = narrow[0]
    lane = iota((NARROW, LANES), 1)
    src = iota((NARROW, LANES), 0)
    labels = recv[pl.ds(2 * CAP, NARROW, stride=UNIT), :]
    raw = recv[pl.ds(2 * CAP + 1, NARROW, stride=UNIT), :]
    code = labels.astype(I32)
    plain = (code - 1) % AGG
    plain = jnp.where(code > 0, plain, -1)

    cells = jnp.where(lane % 16 < 8, raw, pltpu.roll(raw, NARROW - 1, 0))
    data, source = interface_level(cells)
    field = data.start(source, 2)
    mis = [pltpu.roll(m, LANES - 8, 1) for m in data.misfit(field, source)]
    mis = jnp.concatenate(mis, axis=1)
    wide_lane = iota((NARROW, 2 * LANES), 1) % LANES
    real = iota((NARROW, 2 * LANES), 0) < NARROW - 1
    after_end = jnp.where((wide_lane >= LANES - 3) & real, mis, 0.0)
    at_start = jnp.where((wide_lane < 3) & real, mis, 0.0)
    is_end = (code > 128) & (lane < CAP)
    is_start = (code > 64) & (code <= 128) & (lane < CAP)
    end_at = jnp.max(jnp.where(is_end, plain, -1), axis=1, keepdims=True)
    start_at = jnp.max(jnp.where(is_start, plain, -1), axis=1, keepdims=True)
    end_hot = jnp.where(lane == end_at, 1.0, 0.0)
    start_hot = jnp.where(lane == start_at, 1.0, 0.0)
    start_next = pltpu.roll(start_hot, NARROW - 1, 0)
    zeros = jnp.zeros((2 * NARROW, LANES), F32)
    hot = jnp.transpose(jnp.concatenate([end_hot, start_next, zeros], axis=0), (1, 0))
    edge_hot = hot[0:AGG, :].astype(BF16)
    edge_rows = jnp.concatenate(
        [after_end, at_start, jnp.zeros((2 * NARROW, 2 * LANES), F32)], axis=0
    )

    rows = []
    for t in range(NARROW // 8):
        mine = jnp.where(lane[0:8] // CAP == src[0:8], plain[8 * t : 8 * t + 8], 0)
        rows.append(jnp.sum(mine, axis=0, keepdims=True))
    total = select_rows(edge_hot, edge_rows)
    for half in (0, 1):
        hots, parts = [], []
        for t in (2 * half, 2 * half + 1):
            hots.append(iota((AGG, LANES), 0) == rows[t])
            for s in range(8 * t, 8 * t + 8):
                parts.append(
                    jnp.concatenate(
                        [recv[pl.ds(s * UNIT + f, CAP, stride=2), :] for f in (0, 1)], axis=1
                    )
                )
        total = total + select_rows(
            as_bf16(jnp.concatenate(hots, axis=1)), jnp.concatenate(parts, axis=0)
        )
    source_c = [total[:, 0:LANES], total[:, LANES:]]
    level = coarse_level(coef)
    correction = level.start(source_c, 2)
    store2(leftover, level.misfit(correction, source_c))
    store2(below, correction)
    store2(source_out, source_c)

    for t in range(NARROW // 8):
        marks[t : t + 1, :] = rows[t].astype(F32)
    marks[8 : 8 + NARROW, :] = pltpu.roll(end_hot, 1, 0)
    marks[8 + NARROW : 8 + 2 * NARROW, :] = start_next
    own_edges[0:1, :] = jnp.sum(jnp.where(src == n - 1, cells, 0.0), axis=0, keepdims=True)
    own_edges[1:2, :] = jnp.sum(jnp.where(src == n, cells, 0.0), axis=0, keepdims=True)


def second_kernel(mine, other, coef, leftover, below, source_out):
    source = [a + b for a, b in zip(load2(mine), load2(other))]
    level = coarse_level(coef)
    correction = level.start(source, 2)
    store2(leftover, level.misfit(correction, source))
    store2(below, correction)
    store2(source_out, source)


def top_kernel(
    left2, left2_a, left2_b, left2_c,
    coef2, coef2_a, coef2_b, coef2_c,
    below2, source2, coef1, below1, source1, marks, out, near, far, top,
):
    near[...] = coef2[...] + coef2_a[...]
    far[...] = coef2_b[...] + coef2_c[...]
    top[...] = near[...] + far[...]
    source3 = [a + b for a, b in zip(load2(left2), load2(left2_a))]
    source3_far = [a + b for a, b in zip(load2(left2_b), load2(left2_c))]
    level3, level3_far, level4 = coarse_level(near), coarse_level(far), coarse_level(top)
    below3 = level3.start(source3, 2)
    below3_far = level3_far.start(source3_far, 2)
    source4 = [
        a + b
        for a, b in zip(
            level3.misfit(below3, source3), level3_far.misfit(below3_far, source3_far)
        )
    ]
    v = level4.start(source4, 4)
    v = level3.smooth([a + b for a, b in zip(below3, v)], source3, 2)
    v = coarse_level(coef2).smooth([a + b for a, b in zip(load2(below2), v)], load2(source2), 2)
    v = coarse_level(coef1).smooth([a + b for a, b in zip(load2(below1), v)], load2(source1), 2)

    both = jnp.concatenate([v[0], v[1]], axis=1)
    both = jnp.concatenate([both, jnp.zeros((LANES - AGG, 2 * LANES), F32)], axis=0)
    lane = iota((LANES, LANES), 1)
    for t in range(NARROW // 8):
        mark = jnp.broadcast_to(marks[t : t + 1, :], (LANES, LANES))
        hot = as_bf16(jnp.transpose(mark, (1, 0)).astype(I32) == lane)
        rows = select_rows(hot, both)
        for s in range(8):
            for f in (0, 1):
                out[pl.ds((8 * t + s) * UNIT + f, CAP, stride=2), :] = rows[
                    s * CAP : (s + 1) * CAP, f * LANES : (f + 1) * LANES
                ]
    ends = select_rows(marks[8 : 8 + 2 * NARROW, :].astype(BF16), both)
    for f in (0, 1):
        part = ends[:, f * LANES : (f + 1) * LANES]
        out[pl.ds(2 * CAP + f, NARROW, stride=UNIT), :] = jnp.where(
            iota((NARROW, LANES), 1) >= LANES // 2, part[0:NARROW], part[NARROW:]
        )


def post_kernel(narrow, rhs, face, sink, kap, mask, slots, recv, own_edges, out):
    n = narrow[0]
    data, source = fine_inputs(rhs, face, sink, kap, mask)
    field = data.start(source, 2)
    slot = slots[...].astype(I32)
    lane = iota((BLK, LANES), 1)
    lifted = None
    for half in (0, 1):
        hots, parts = [], []
        for t in (2 * half, 2 * half + 1):
            hots.append(slot == lane + t * LANES)
            for s in range(8 * t, 8 * t + 8):
                parts.append(
                    jnp.concatenate(
                        [recv[pl.ds(s * UNIT + f, CAP, stride=2), :] for f in (0, 1)], axis=1
                    )
                )
        term = select_rows(as_bf16(jnp.concatenate(hots, axis=1)), jnp.concatenate(parts, axis=0))
        lifted = term if lifted is None else lifted + term
    lifted = [lifted[:, 0:LANES], lifted[:, LANES:]]
    v = data.smooth([a + b for a, b in zip(field, lifted)], source, 2)

    edge_data, edge_source = interface_level(own_edges[...])
    edge_field = edge_data.start(edge_source, 2)
    lane1 = iota((1, LANES), 1)
    row8 = iota((8, LANES), 0)
    edge_v = []
    for f in (0, 1):
        beyond = jnp.sum(recv[pl.ds(2 * CAP + f, NARROW, stride=UNIT), :], axis=0, keepdims=True)
        first = jnp.where(lane1 >= LANES // 2, beyond, lifted[f][0:1, :])
        final = jnp.where(lane1 >= LANES // 2, lifted[f][BLK - 1 : BLK, :], beyond)
        lift = jnp.where(row8 == 0, first, jnp.where(row8 == 1, final, 0.0))
        lift = jnp.where(iota((8, LANES), 1) < 16, pltpu.roll(lift, 8, 1), 0.0)
        edge_v.append(edge_field[f] + lift)
    edge_v = edge_data.smooth(edge_v, edge_source, 2)
    for f in (0, 1):
        out[pl.ds(f, BLK, stride=2), :] = v[f]
        moved = pltpu.roll(edge_v[f], LANES - 8, 1)
        out[f : f + 1, :] = jnp.where((lane1 < 4) & (n > 0), moved[0:1, :], v[f][0:1, :])
        final = 2 * (BLK - 1) + f
        out[final : final + 1, :] = jnp.where(
            (lane1 >= LANES - 4) & (n < NARROW - 1), moved[1:2, :], v[f][BLK - 1 : BLK, :]
        )


def call(kernel, outs, *args, smem=0, scratch=()):
    space = lambda k: pltpu.SMEM if k < smem else pltpu.VMEM
    return pl.pallas_call(
        kernel,
        out_shape=[jax.ShapeDtypeStruct(s, F32) for s in outs],
        in_specs=[pl.BlockSpec(memory_space=space(k)) for k in range(len(args))],
        out_specs=[pl.BlockSpec(memory_space=pltpu.VMEM) for _ in outs],
        scratch_shapes=[pltpu.VMEM(s, F32) for s in scratch],
        compiler_params=pltpu.CompilerParams(vmem_limit_bytes=32 * 1024 * 1024),
    )(*args)


def exchange(value, bits):
    return lax.ppermute(value, "wide", [(i, i ^ bits) for i in range(lax.axis_size("wide"))])


def to_all(units):
    shape = (NARROW * UNIT // 2, 2, LANES)
    moved = lax.all_to_all(units.reshape(shape), "narrow", 0, 0, tiled=True)
    return moved.reshape(NARROW * UNIT, LANES)


def on_device(
    rhs, fine_face, fine_sink, fine_kap, cell_mask, block_aggregate, coarse_face, coarse_sink, coarse_kap
):
    narrow = lax.axis_index("narrow").astype(I32).reshape(1)
    fine = (
        rhs.reshape(2 * BLK, LANES),
        fine_face.reshape(2 * BLK, LANES),
        fine_sink.reshape(2 * BLK, LANES),
        fine_kap,
        cell_mask,
    )
    five, two, units = (5 * AGG, LANES), (2 * AGG, LANES), (NARROW * UNIT, LANES)
    (coef1,) = call(
        coef_kernel,
        [five],
        coarse_face.reshape(2 * AGG, LANES),
        coarse_sink.reshape(2 * AGG, LANES),
        coarse_kap,
    )
    coef2 = coef1 + exchange(coef1, 1)
    coef2_x = [exchange(coef2, b) for b in (2, 4, 6)]

    sent, slots = call(
        pre_kernel,
        [units, (BLK, LANES)],
        narrow,
        *fine,
        block_aggregate.reshape(1, BLK),
        smem=1,
    )
    recv = to_all(sent)
    left1, below1, source1, marks, own_edges = call(
        restrict_kernel,
        [two, two, two, (8 + 2 * NARROW, LANES), (8, LANES)],
        narrow,
        recv,
        coef1,
        smem=1,
    )
    left2, below2, source2 = call(
        second_kernel, [two, two, two], left1, exchange(left1, 1), coef2
    )
    left2_x = [exchange(left2, b) for b in (2, 4, 6)]
    (back,) = call(
        top_kernel,
        [units],
        left2, *left2_x, coef2, *coef2_x, below2, source2, coef1, below1, source1, marks,
        scratch=(five, five, five),
    )
    recv = to_all(back)
    (out,) = call(
        post_kernel, [(2 * BLK, LANES)], narrow, *fine, slots, recv, own_edges, smem=1
    )
    return out.reshape(BLK, 2, LANES)


def solution(mesh):
    both = ("wide", "narrow")
    placed = (
        P(both, None, None),
        P(both, None, None),
        P(both, None, None),
        P(both, None),
        P(both, None),
        P(both),
        P(both, None, None),
        P(both, None, None),
        P(both, None),
    )
    return jax.shard_map(
        on_device,
        mesh=mesh,
        in_specs=placed,
        out_specs=P(both, None, None),
        check_vma=False,
    )
```

```python
import jax
import jax.numpy as jnp
from jax import lax
from jax.experimental import pallas as pl
from jax.experimental.pallas import tpu as pltpu
from jax.sharding import PartitionSpec as P

OMEGA = 0.8
LANES = 128
BLK = 256
AGG = 64
NARROW = 32
CAP = 16
UNIT = 2 * (CAP + 1)
F32, BF16, I32 = jnp.float32, jnp.bfloat16, jnp.int32


def iota(shape, dim):
    return lax.broadcasted_iota(I32, shape, dim)


def chain_next(v):
    ahead = pltpu.roll(v, LANES - 1, 1)
    below = pltpu.roll(ahead, v.shape[0] - 1, 0)
    return jnp.where(iota(v.shape, 1) == LANES - 1, below, ahead)


def chain_prev(v):
    behind = pltpu.roll(v, 1, 1)
    above = pltpu.roll(behind, 1, 0)
    return jnp.where(iota(v.shape, 1) == 0, above, behind)


def row_next(v):
    return pltpu.roll(v, LANES - 1, 1)


def row_prev(v):
    return pltpu.roll(v, 1, 1)


class Level:
    def __init__(self, faces, sinks, coupling, prev, nxt):
        self.prev, self.nxt = prev, nxt
        self.faces = faces
        self.left = [prev(f) for f in faces]
        self.diag = [s + l + f for s, l, f in zip(sinks, self.left, faces)]
        self.coupling = coupling
        scale = OMEGA / (self.diag[0] * self.diag[1] - coupling * coupling)
        self.inv = (self.diag[1] * scale, self.diag[0] * scale, coupling * scale)

    def parts(self):
        return [*self.faces, *self.left, *self.diag, self.coupling, *self.inv]

    @classmethod
    def load(cls, part, prev, nxt):
        level = cls.__new__(cls)
        level.prev, level.nxt = prev, nxt
        level.faces, level.left, level.diag = part[0:2], part[2:4], part[4:6]
        level.coupling, level.inv = part[6], part[7:10]
        return level

    def misfit(self, v, source):
        return [
            source[f]
            - (
                self.diag[f] * v[f]
                - self.left[f] * self.prev(v[f])
                - self.faces[f] * self.nxt(v[f])
                - self.coupling * v[1 - f]
            )
            for f in (0, 1)
        ]

    def step(self, r):
        return [
            self.inv[0] * r[0] + self.inv[2] * r[1],
            self.inv[2] * r[0] + self.inv[1] * r[1],
        ]

    def smooth(self, v, source, sweeps):
        for _ in range(sweeps):
            d = self.step(self.misfit(v, source))
            v = [v[0] + d[0], v[1] + d[1]]
        return v

    def start(self, source, sweeps):
        return self.smooth(self.step(source), source, sweeps - 1)


def fine_level(face, sink, kap, live, prev, nxt, last):
    live_next = jnp.where(last, 0.0, nxt(live))
    both = live * live_next
    faces = [f * both for f in face]
    coupling = kap * jnp.sqrt(sink[0] * sink[1]) * live
    return Level(faces, sink, coupling, prev, nxt)


def store(ref, parts, at=0):
    for part in parts:
        ref[at : at + part.shape[0], :] = part
        at += part.shape[0]


def load(ref, count, rows, at=0):
    return [ref[at + k * rows : at + (k + 1) * rows, :] for k in range(count)]


def last_cell(shape):
    return (iota(shape, 0) == shape[0] - 1) & (iota(shape, 1) == LANES - 1)


def split3(x):
    hi = x.astype(BF16)
    rest = x - hi.astype(F32)
    mid = rest.astype(BF16)
    return hi, mid, (rest - mid.astype(F32)).astype(BF16)


def select_rows(onehot, x):
    total = None
    for part in split3(x):
        term = jnp.dot(onehot, part, preferred_element_type=F32)
        total = term if total is None else total + term
    return total


def as_bf16(mask):
    return jnp.where(mask, 1.0, 0.0).astype(BF16)


def planar(ref, rows):
    return [ref[pl.ds(f, rows, stride=2), :] for f in (0, 1)]


def start_copies(sources, targets, sems):
    copies = [
        pltpu.make_async_copy(a, b, sems.at[k]) for k, (a, b) in enumerate(zip(sources, targets))
    ]
    for copy in copies:
        copy.start()
    return copies


def fine_start(rhs, face, sink, kap, mask):
    live = mask[...].astype(F32)
    data = fine_level(
        planar(face, BLK), planar(sink, BLK), kap[...], live, chain_prev, chain_next, last_cell((BLK, LANES))
    )
    source = [r * live for r in planar(rhs, BLK)]
    return data, source, data.start(source, 2)


def ready_kernel(token, *refs):
    inputs, fine, held, sems = refs[0:5], refs[5], refs[6:11], refs[11]
    for copy in start_copies(inputs, held, sems):
        copy.wait()
    data, source, field = fine_start(*held)
    store(fine, [*field, *source, *data.parts()])


def pre_kernel(narrow, agg_hbm, *refs):
    inputs, out, slots, held, sems = refs[0:5], refs[5], refs[6], refs[7:13], refs[13]
    rhs, face, sink, kap, mask, agg = held
    n = narrow[0]
    copies = start_copies((*inputs, agg_hbm), held, sems)
    copies.pop().wait()

    label = agg[...]
    owner = label // AGG
    within = label - owner * AGG
    owned = iota((NARROW, BLK), 0) == owner
    before = as_bf16(iota((BLK, BLK), 0) < iota((BLK, BLK), 1))
    counts = jnp.dot(as_bf16(owned), before, preferred_element_type=F32)
    rank = jnp.sum(jnp.where(owned, counts, 0.0), axis=0, keepdims=True).astype(I32)
    slot = owner * CAP + rank
    put = as_bf16(iota((NARROW * CAP, BLK), 0) == slot)

    block = iota((1, BLK), 1)
    code = within + 1 + jnp.where(block == 0, 64, 0) + jnp.where(block == BLK - 1, 128, 0)
    coded = jnp.where(owned, code.astype(F32), 0.0).astype(BF16)
    at_rank = as_bf16(iota((LANES, BLK), 0) % CAP == rank)
    labels = lax.dot_general(
        coded, at_rank, (((1,), (1,)), ((), ())), preferred_element_type=F32
    )
    out[pl.ds(2 * CAP, NARROW, stride=UNIT), :] = labels
    slots[...] = jnp.transpose(jnp.broadcast_to(slot.astype(F32), (LANES, BLK)), (1, 0))

    for copy in copies:
        copy.wait()
    data, source, field = fine_start(rhs, face, sink, kap, mask)
    misfit = data.misfit(field, source)
    row, lane = iota((BLK, LANES), 0), iota((BLK, LANES), 1)
    drop = ((row == BLK - 1) & (lane >= LANES - 3) & (n < NARROW - 1)) | (
        (row == 0) & (lane < 3) & (n > 0)
    )
    misfit = jnp.concatenate([jnp.where(drop, 0.0, m) for m in misfit], axis=1)

    rows = select_rows(put, misfit)
    for o in range(NARROW):
        for f in (0, 1):
            out[pl.ds(o * UNIT + f, CAP, stride=2), :] = rows[
                o * CAP : (o + 1) * CAP, f * LANES : (f + 1) * LANES
            ]

    lane1 = iota((1, LANES), 1)
    edges = jnp.zeros((1, LANES), F32)
    quantities = [(ref, 2, f) for ref in (rhs, face, sink) for f in (0, 1)]
    quantities += [(kap, 1, 0), (mask, 1, 0)]
    for q, (ref, stride, f) in enumerate(quantities):
        final = (BLK - 1) * stride + f
        cells = jnp.where(
            lane1 >= LANES // 2, ref[final : final + 1, :], ref[f : f + 1, :]
        ).astype(F32)
        moved = pltpu.roll(cells, (16 * q + 8) % LANES, 1)
        edges = jnp.where(lane1 // 16 == q, moved, edges)
    out[pl.ds(2 * CAP + 1, NARROW, stride=UNIT), :] = jnp.broadcast_to(edges, (NARROW, LANES))


def interface_level(cells):
    lane = iota(cells.shape, 1)

    def quantity(q, fill):
        moved = cells if q == 0 else pltpu.roll(cells, LANES - 16 * q, 1)
        return jnp.where(lane < 16, moved, fill)

    rhs = [quantity(0, 0.0), quantity(1, 0.0)]
    face = [quantity(2, 0.0), quantity(3, 0.0)]
    sink = [quantity(4, 1.0), quantity(5, 1.0)]
    kap, live = quantity(6, 0.0), quantity(7, 0.0)
    data = fine_level(face, sink, kap, live, row_prev, row_next, lane == LANES - 1)
    source = [r * live for r in rhs]
    return data, source


PARTS = 10


def coarse_level(ref):
    part = load(ref, 5, AGG)
    return Level(part[0:2], part[2:4], part[4], chain_prev, chain_next)


def ready_level(ref, at=0):
    return Level.load(load(ref, PARTS, AGG, at * PARTS * AGG), chain_prev, chain_next)


def store2(ref, v):
    ref[0:AGG, :] = v[0]
    ref[AGG : 2 * AGG, :] = v[1]


def load2(ref):
    return [ref[0:AGG, :], ref[AGG : 2 * AGG, :]]


def coef_kernel(token, face_hbm, sink_hbm, kap_hbm, out, level, face, sink, kap, sems):
    for copy in start_copies((face_hbm, sink_hbm, kap_hbm), (face, sink, kap), sems):
        copy.wait()
    faces, sinks = planar(face, AGG), planar(sink, AGG)
    last = last_cell((AGG, LANES))
    for f in (0, 1):
        out[f * AGG : (f + 1) * AGG, :] = jnp.where(last, 0.0, faces[f])
        out[(2 + f) * AGG : (3 + f) * AGG, :] = sinks[f]
    out[4 * AGG : 5 * AGG, :] = kap[...] * jnp.sqrt(sinks[0] * sinks[1])
    store(level, coarse_level(out).parts())


def pair_kernel(mine, other, out, level):
    out[...] = mine[...] + other[...]
    store(level, coarse_level(out).parts())


def upper_kernel(coef2, coef2_a, coef2_b, coef2_c, levels, near, far, top):
    near[...] = coef2[...] + coef2_a[...]
    far[...] = coef2_b[...] + coef2_c[...]
    top[...] = near[...] + far[...]
    for k, ref in enumerate((near, far, top)):
        store(levels, coarse_level(ref).parts(), k * PARTS * AGG)


def restrict_kernel(narrow, recv, level1, token, leftover, below, source_out, marks, own_edges):
    n = narrow[0]
    lane = iota((NARROW, LANES), 1)
    src = iota((NARROW, LANES), 0)
    labels = recv[pl.ds(2 * CAP, NARROW, stride=UNIT), :]
    raw = recv[pl.ds(2 * CAP + 1, NARROW, stride=UNIT), :]
    code = labels.astype(I32)
    plain = (code - 1) % AGG
    plain = jnp.where(code > 0, plain, -1)

    cells = jnp.where(lane % 16 < 8, raw, pltpu.roll(raw, NARROW - 1, 0))
    data, source = interface_level(cells)
    field = data.start(source, 2)
    mis = [pltpu.roll(m, LANES - 8, 1) for m in data.misfit(field, source)]
    mis = jnp.concatenate(mis, axis=1)
    wide_lane = iota((NARROW, 2 * LANES), 1) % LANES
    real = iota((NARROW, 2 * LANES), 0) < NARROW - 1
    after_end = jnp.where((wide_lane >= LANES - 3) & real, mis, 0.0)
    at_start = jnp.where((wide_lane < 3) & real, mis, 0.0)
    is_end = (code > 128) & (lane < CAP)
    is_start = (code > 64) & (code <= 128) & (lane < CAP)
    end_at = jnp.max(jnp.where(is_end, plain, -1), axis=1, keepdims=True)
    start_at = jnp.max(jnp.where(is_start, plain, -1), axis=1, keepdims=True)
    end_hot = jnp.where(lane == end_at, 1.0, 0.0)
    start_hot = jnp.where(lane == start_at, 1.0, 0.0)
    start_next = pltpu.roll(start_hot, NARROW - 1, 0)
    zeros = jnp.zeros((2 * NARROW, LANES), F32)
    hot = jnp.transpose(jnp.concatenate([end_hot, start_next, zeros], axis=0), (1, 0))
    edge_hot = hot[0:AGG, :].astype(BF16)
    edge_rows = jnp.concatenate(
        [after_end, at_start, jnp.zeros((2 * NARROW, 2 * LANES), F32)], axis=0
    )

    rows = []
    for t in range(NARROW // 8):
        mine = jnp.where(lane[0:8] // CAP == src[0:8], plain[8 * t : 8 * t + 8], 0)
        rows.append(jnp.sum(mine, axis=0, keepdims=True))
    total = select_rows(edge_hot, edge_rows)
    for half in (0, 1):
        hots, parts = [], []
        for t in (2 * half, 2 * half + 1):
            hots.append(iota((AGG, LANES), 0) == rows[t])
            for s in range(8 * t, 8 * t + 8):
                parts.append(
                    jnp.concatenate(
                        [recv[pl.ds(s * UNIT + f, CAP, stride=2), :] for f in (0, 1)], axis=1
                    )
                )
        total = total + select_rows(
            as_bf16(jnp.concatenate(hots, axis=1)), jnp.concatenate(parts, axis=0)
        )
    source_c = [total[:, 0:LANES], total[:, LANES:]]
    level = ready_level(level1)
    correction = level.start(source_c, 2)
    store2(leftover, level.misfit(correction, source_c))
    store2(below, correction)
    store2(source_out, source_c)

    for t in range(NARROW // 8):
        marks[t : t + 1, :] = rows[t].astype(F32)
    marks[8 : 8 + NARROW, :] = pltpu.roll(end_hot, 1, 0)
    marks[8 + NARROW : 8 + 2 * NARROW, :] = start_next
    own_edges[0:1, :] = jnp.sum(jnp.where(src == n - 1, cells, 0.0), axis=0, keepdims=True)
    own_edges[1:2, :] = jnp.sum(jnp.where(src == n, cells, 0.0), axis=0, keepdims=True)


def second_kernel(mine, other, level2, leftover, below, source_out):
    source = [a + b for a, b in zip(load2(mine), load2(other))]
    level = ready_level(level2)
    correction = level.start(source, 2)
    store2(leftover, level.misfit(correction, source))
    store2(below, correction)
    store2(source_out, source)


def side_kernel(marks, own_edges, hot, edges):
    lane = iota((LANES, LANES), 1)
    for t in range(NARROW // 8):
        mark = jnp.broadcast_to(marks[t : t + 1, :], (LANES, LANES))
        mark = jnp.transpose(mark, (1, 0)).astype(I32)
        once = as_bf16(mark == lane % AGG)
        last = as_bf16((mark == lane) & (lane < AGG))
        hot[t * LANES : (t + 1) * LANES, 0:LANES] = once
        hot[t * LANES : (t + 1) * LANES, LANES:] = last
    ends = marks[8 : 8 + 2 * NARROW, :]
    hot[NARROW * CAP :, 0:LANES] = (ends + pltpu.roll(ends, AGG, 1)).astype(BF16)
    hot[NARROW * CAP :, LANES:] = ends.astype(BF16)
    data, source = interface_level(own_edges[...])
    field = data.start(source, 2)
    store(edges, [*field, *source, *data.parts()])


def top_kernel(
    left2, left2_a, left2_b, left2_c, levels, level2, below2, source2, level1, below1, source1, hot, out
):
    source3 = [a + b for a, b in zip(load2(left2), load2(left2_a))]
    source3_far = [a + b for a, b in zip(load2(left2_b), load2(left2_c))]
    level3, level3_far, level4 = [ready_level(levels, k) for k in range(3)]
    below3 = level3.start(source3, 2)
    below3_far = level3_far.start(source3_far, 2)
    source4 = [
        a + b
        for a, b in zip(
            level3.misfit(below3, source3), level3_far.misfit(below3_far, source3_far)
        )
    ]
    v = level4.start(source4, 4)
    v = level3.smooth([a + b for a, b in zip(below3, v)], source3, 2)
    v = ready_level(level2).smooth([a + b for a, b in zip(load2(below2), v)], load2(source2), 2)
    v = ready_level(level1).smooth([a + b for a, b in zip(load2(below1), v)], load2(source1), 2)

    both = jnp.concatenate([v[0], v[1]], axis=1)
    both = jnp.concatenate([*split3(both), jnp.zeros((AGG, 2 * LANES), BF16)], axis=0)
    rows = jnp.dot(hot[...], both, preferred_element_type=F32)
    for s in range(NARROW):
        for f in (0, 1):
            out[pl.ds(s * UNIT + f, CAP, stride=2), :] = rows[
                s * CAP : (s + 1) * CAP, f * LANES : (f + 1) * LANES
            ]
    ends = rows[NARROW * CAP :, :]
    for f in (0, 1):
        part = ends[:, f * LANES : (f + 1) * LANES]
        out[pl.ds(2 * CAP + f, NARROW, stride=UNIT), :] = jnp.where(
            iota((NARROW, LANES), 1) >= LANES // 2, part[0:NARROW], part[NARROW:]
        )


def post_kernel(narrow, fine, slots, recv, edges, out):
    n = narrow[0]
    field, source = load(fine, 2, BLK), load(fine, 2, BLK, 2 * BLK)
    data = Level.load(load(fine, PARTS, BLK, 4 * BLK), chain_prev, chain_next)
    slot = slots[...].astype(I32)
    lane = iota((BLK, LANES), 1)
    lifted = None
    for half in (0, 1):
        hots, parts = [], []
        for t in (2 * half, 2 * half + 1):
            hots.append(slot == lane + t * LANES)
            for s in range(8 * t, 8 * t + 8):
                parts.append(
                    jnp.concatenate(
                        [recv[pl.ds(s * UNIT + f, CAP, stride=2), :] for f in (0, 1)], axis=1
                    )
                )
        term = select_rows(as_bf16(jnp.concatenate(hots, axis=1)), jnp.concatenate(parts, axis=0))
        lifted = term if lifted is None else lifted + term
    lifted = [lifted[:, 0:LANES], lifted[:, LANES:]]
    v = data.smooth([a + b for a, b in zip(field, lifted)], source, 2)

    edge_field, edge_source = load(edges, 2, 8), load(edges, 2, 8, 16)
    edge_data = Level.load(load(edges, PARTS, 8, 32), row_prev, row_next)
    lane1 = iota((1, LANES), 1)
    row8 = iota((8, LANES), 0)
    edge_v = []
    for f in (0, 1):
        beyond = jnp.sum(recv[pl.ds(2 * CAP + f, NARROW, stride=UNIT), :], axis=0, keepdims=True)
        first = jnp.where(lane1 >= LANES // 2, beyond, lifted[f][0:1, :])
        final = jnp.where(lane1 >= LANES // 2, lifted[f][BLK - 1 : BLK, :], beyond)
        lift = jnp.where(row8 == 0, first, jnp.where(row8 == 1, final, 0.0))
        lift = jnp.where(iota((8, LANES), 1) < 16, pltpu.roll(lift, 8, 1), 0.0)
        edge_v.append(edge_field[f] + lift)
    edge_v = edge_data.smooth(edge_v, edge_source, 2)
    for f in (0, 1):
        out[pl.ds(f, BLK, stride=2), :] = v[f]
        moved = pltpu.roll(edge_v[f], LANES - 8, 1)
        out[f : f + 1, :] = jnp.where((lane1 < 4) & (n > 0), moved[0:1, :], v[f][0:1, :])
        final = 2 * (BLK - 1) + f
        out[final : final + 1, :] = jnp.where(
            (lane1 >= LANES - 4) & (n < NARROW - 1), moved[1:2, :], v[f][BLK - 1 : BLK, :]
        )


def call(kernel, outs, *args, spaces=(), scratch=(), cost=None):
    spaces = (*spaces, *[pltpu.VMEM] * (len(args) - len(spaces)))
    args = [
        pltpu.with_memory_space_constraint(a, s) if s == pltpu.HBM else a
        for a, s in zip(args, spaces)
    ]
    return pl.pallas_call(
        kernel,
        out_shape=[jax.ShapeDtypeStruct(s, k) for s, k in outs],
        in_specs=[pl.BlockSpec(memory_space=space) for space in spaces],
        out_specs=[pl.BlockSpec(memory_space=pltpu.VMEM) for _ in outs],
        scratch_shapes=scratch,
        cost_estimate=cost,
        compiler_params=pltpu.CompilerParams(vmem_limit_bytes=32 * 1024 * 1024),
    )(*args)


def exchange(value, bits):
    return lax.ppermute(value, "wide", [(i, i ^ bits) for i in range(lax.axis_size("wide"))])


def to_all(units):
    shape = (NARROW * UNIT // 2, 2, LANES)
    moved = lax.all_to_all(units.reshape(shape), "narrow", 0, 0, tiled=True)
    return moved.reshape(NARROW * UNIT, LANES)


def on_device(
    rhs, fine_face, fine_sink, fine_kap, cell_mask, block_aggregate, coarse_face, coarse_sink, coarse_kap
):
    narrow = lax.axis_index("narrow").astype(I32).reshape(1)
    cells = ((2 * BLK, LANES), F32)
    five, level, two = ((k * AGG, LANES) for k in (5, PARTS, 2))
    five, level, two = (five, F32), (level, F32), (two, F32)
    units = ((NARROW * UNIT, LANES), F32)
    vmem = lambda *rows: [pltpu.VMEM((r, LANES), F32) for r in rows]
    held = vmem(2 * BLK, 2 * BLK, 2 * BLK, BLK) + [pltpu.VMEM((BLK, LANES), I32)]
    beside = pl.CostEstimate(flops=0, bytes_accessed=4 * 1024 * 1024, transcendentals=0)
    fine_args = (
        rhs.reshape(2 * BLK, LANES),
        fine_face.reshape(2 * BLK, LANES),
        fine_sink.reshape(2 * BLK, LANES),
        fine_kap,
        cell_mask,
    )
    sent, slots = call(
        pre_kernel,
        [units, ((BLK, LANES), F32)],
        narrow,
        block_aggregate.reshape(1, BLK),
        *fine_args,
        spaces=(pltpu.SMEM, *[pltpu.HBM] * 6),
        scratch=held + [pltpu.VMEM((1, BLK), I32), pltpu.SemaphoreType.DMA((6,))],
    )
    recv = to_all(sent)
    coef1, level1 = call(
        coef_kernel,
        [five, level],
        slots,
        coarse_face.reshape(2 * AGG, LANES),
        coarse_sink.reshape(2 * AGG, LANES),
        coarse_kap,
        spaces=(pltpu.VMEM, *[pltpu.HBM] * 3),
        scratch=vmem(2 * AGG, 2 * AGG, AGG) + [pltpu.SemaphoreType.DMA((3,))],
        cost=beside,
    )
    (fine,) = call(
        ready_kernel,
        [((14 * BLK, LANES), F32)],
        slots,
        *fine_args,
        spaces=(pltpu.VMEM, *[pltpu.HBM] * 5),
        scratch=held + [pltpu.SemaphoreType.DMA((5,))],
        cost=beside,
    )
    coef2, level2 = call(pair_kernel, [five, level], coef1, exchange(coef1, 1), cost=beside)
    (levels,) = call(
        upper_kernel,
        [((3 * PARTS * AGG, LANES), F32)],
        coef2,
        *[exchange(coef2, b) for b in (2, 6, 4)],
        scratch=vmem(5 * AGG, 5 * AGG, 5 * AGG),
        cost=beside,
    )
    left1, below1, source1, marks, own_edges = call(
        restrict_kernel,
        [two, two, two, ((8 + 2 * NARROW, LANES), F32), ((8, LANES), F32)],
        narrow,
        recv,
        level1,
        fine,
        spaces=(pltpu.SMEM,),
    )
    hot, edges = call(
        side_kernel,
        [((NARROW * CAP + 2 * NARROW, 2 * LANES), BF16), ((14 * 8, LANES), F32)],
        marks,
        own_edges,
    )
    left2, below2, source2 = call(
        second_kernel, [two, two, two], left1, exchange(left1, 1), level2
    )
    (back,) = call(
        top_kernel,
        [units],
        left2,
        *[exchange(left2, b) for b in (2, 6, 4)],
        levels,
        level2,
        below2,
        source2,
        level1,
        below1,
        source1,
        hot,
    )
    recv = to_all(back)
    (out,) = call(post_kernel, [cells], narrow, fine, slots, recv, edges, spaces=(pltpu.SMEM,))
    return out.reshape(BLK, 2, LANES)


def solution(mesh):
    both = ("wide", "narrow")
    placed = (
        P(both, None, None),
        P(both, None, None),
        P(both, None, None),
        P(both, None),
        P(both, None),
        P(both),
        P(both, None, None),
        P(both, None, None),
        P(both, None),
    )
    return jax.shard_map(
        on_device,
        mesh=mesh,
        in_specs=placed,
        out_specs=P(both, None, None),
        check_vma=False,
    )
```

```python
import jax
import jax.numpy as jnp
from jax import lax
from jax.experimental import pallas as pl
from jax.experimental.pallas import tpu as pltpu
from jax.sharding import PartitionSpec as P

OMEGA = 0.8
LANES = 128
BLK = 256
AGG = 64
NARROW = 32
CAP = 16
UNIT = 2 * CAP + 1
SIDE = 7
LABEL = LANES - CAP
F32, BF16, I32 = jnp.float32, jnp.bfloat16, jnp.int32


def iota(shape, dim):
    return lax.broadcasted_iota(I32, shape, dim)


def chain_next(v):
    ahead = pltpu.roll(v, LANES - 1, 1)
    below = pltpu.roll(ahead, v.shape[0] - 1, 0)
    return jnp.where(iota(v.shape, 1) == LANES - 1, below, ahead)


def chain_prev(v):
    behind = pltpu.roll(v, 1, 1)
    above = pltpu.roll(behind, 1, 0)
    return jnp.where(iota(v.shape, 1) == 0, above, behind)


def row_next(v):
    return pltpu.roll(v, LANES - 1, 1)


def row_prev(v):
    return pltpu.roll(v, 1, 1)


class Level:
    def __init__(self, faces, sinks, coupling, prev, nxt, left=None):
        self.prev, self.nxt = prev, nxt
        self.faces = faces
        self.left = [prev(f) for f in faces] if left is None else left
        self.diag = [s + l + f for s, l, f in zip(sinks, self.left, faces)]
        self.coupling = coupling
        scale = OMEGA / (self.diag[0] * self.diag[1] - coupling * coupling)
        self.inv = (self.diag[1] * scale, self.diag[0] * scale, coupling * scale)

    def parts(self):
        return [*self.faces, *self.left, *self.inv, *self.diag, self.coupling]

    @classmethod
    def load(cls, part, prev, nxt):
        level = cls.__new__(cls)
        level.prev, level.nxt = prev, nxt
        level.faces, level.left, level.inv = part[0:2], part[2:4], part[4:7]
        if len(part) > 7:
            level.diag, level.coupling = part[7:9], part[9]
        return level

    def flow(self, v):
        return [self.left[f] * self.prev(v[f]) + self.faces[f] * self.nxt(v[f]) for f in (0, 1)]

    def misfit(self, v, source):
        cell = [
            (source[f] - self.diag[f] * v[f]) + self.coupling * v[1 - f] for f in (0, 1)
        ]
        return [a + b for a, b in zip(cell, self.flow(v))]

    def step(self, r):
        return [
            self.inv[0] * r[0] + self.inv[2] * r[1],
            self.inv[2] * r[0] + self.inv[1] * r[1],
        ]

    def smooth(self, v, drive, sweeps):
        for _ in range(sweeps):
            d = self.step(self.flow(v))
            v = [((1.0 - OMEGA) * v[f] + drive[f]) + d[f] for f in (0, 1)]
        return v

    def start(self, source, sweeps):
        drive = self.step(source)
        return self.smooth(drive, drive, sweeps - 1), drive


def store(ref, parts, at=0):
    for part in parts:
        ref[at : at + part.shape[0], :] = part
        at += part.shape[0]


def load(ref, count, rows, at=0):
    return [ref[at + k * rows : at + (k + 1) * rows, :] for k in range(count)]


def last_cell(shape):
    return (iota(shape, 0) == shape[0] - 1) & (iota(shape, 1) == LANES - 1)


def split3(x):
    hi = x.astype(BF16)
    rest = x - hi.astype(F32)
    mid = rest.astype(BF16)
    return hi, mid, (rest - mid.astype(F32)).astype(BF16)


def select_rows(onehot, x):
    return jnp.dot(
        jnp.concatenate([onehot] * 3, axis=1),
        jnp.concatenate(split3(x), axis=0),
        preferred_element_type=F32,
    )


def as_bf16(mask):
    return jnp.where(mask, 1.0, 0.0).astype(BF16)


def planar(ref, rows):
    return [ref[pl.ds(f, rows, stride=2), :] for f in (0, 1)]


def start_copies(sources, targets, sems):
    copies = [
        pltpu.make_async_copy(a, b, sems.at[k]) for k, (a, b) in enumerate(zip(sources, targets))
    ]
    for copy in copies:
        copy.start()
    return copies


def fine_start(rhs, face, sink, kap, mask):
    live = mask[...].astype(F32)
    live_next = jnp.where(last_cell((BLK, LANES)), 0.0, chain_next(live))
    both = live * live_next
    sinks = planar(sink, BLK)
    coupling = kap[...] * jnp.sqrt(sinks[0] * sinks[1]) * live
    data = Level([f * both for f in planar(face, BLK)], sinks, coupling, chain_prev, chain_next)
    source = [r * live for r in planar(rhs, BLK)]
    return data, source, *data.start(source, 2)


def ready_kernel(slot_row, *refs):
    inputs, fine, slots, held, sems = refs[0:5], refs[5], refs[6], refs[7:12], refs[12]
    copies = start_copies(inputs, held, sems)
    slots[...] = jnp.transpose(jnp.broadcast_to(slot_row[0:1, :], (LANES, BLK)), (1, 0))
    for copy in copies:
        copy.wait()
    data, _, field, drive = fine_start(*held)
    store(fine, [*field, *drive, *data.parts()[0:7]])


def pre_kernel(narrow, agg_hbm, *refs):
    inputs, out, slots, held, sems = refs[0:5], refs[5], refs[6], refs[7:13], refs[13]
    rhs, face, sink, kap, mask, agg = held
    n = narrow[0]
    for copy in start_copies((*inputs, agg_hbm), held, sems):
        copy.wait()

    label = agg[...]
    owner = label // AGG
    within = label - owner * AGG
    owned = iota((NARROW, BLK), 0) == owner
    before = as_bf16(iota((BLK, BLK), 0) < iota((BLK, BLK), 1))
    counts = jnp.dot(as_bf16(owned), before, preferred_element_type=F32)
    rank = jnp.sum(jnp.where(owned, counts, 0.0), axis=0, keepdims=True).astype(I32)
    slot = owner * CAP + rank
    put = as_bf16(iota((NARROW * CAP, BLK), 0) == slot)

    block = iota((1, BLK), 1)
    code = within + 1 + jnp.where(block == 0, 64, 0) + jnp.where(block == BLK - 1, 128, 0)
    coded = jnp.where(owned, code.astype(F32), 0.0).astype(BF16)
    at_rank = as_bf16(iota((LANES, BLK), 0) % CAP == rank)
    labels = lax.dot_general(
        coded, at_rank, (((1,), (1,)), ((), ())), preferred_element_type=F32
    )
    slots[...] = jnp.broadcast_to(slot.astype(F32), (8, BLK))

    data, source, field, _ = fine_start(rhs, face, sink, kap, mask)
    misfit = data.misfit(field, source)
    row, lane = iota((BLK, LANES), 0), iota((BLK, LANES), 1)
    drop = ((row == BLK - 1) & (lane >= LANES - 3) & (n < NARROW - 1)) | (
        (row == 0) & (lane < 3) & (n > 0)
    )
    misfit = jnp.concatenate([jnp.where(drop, 0.0, m) for m in misfit], axis=1)

    rows = select_rows(put, misfit)
    for o in range(NARROW):
        for f in (0, 1):
            out[pl.ds(o * UNIT + f, CAP, stride=2), :] = rows[
                o * CAP : (o + 1) * CAP, f * LANES : (f + 1) * LANES
            ]

    lane1 = iota((1, LANES), 1)

    def ends(final, first):
        return jnp.where(lane1 >= LANES // 2, final, first)

    def rows_of(v):
        return ends(v[BLK - 1 : BLK, :], v[0:1, :])

    live_first = mask[0:1, :].astype(F32)
    live_final = mask[BLK - 1 : BLK, :].astype(F32)
    faces = []
    for f in (0, 1):
        open_face = face[2 * (BLK - 1) + f : 2 * (BLK - 1) + f + 1, :] * live_final
        final = jnp.where(lane1 == LANES - 1, open_face, data.faces[f][BLK - 1 : BLK, :])
        faces.append(ends(final, data.faces[f][0:1, :]))
    sinks = [
        ends(sink[2 * (BLK - 1) + f : 2 * (BLK - 1) + f + 1, :], sink[f : f + 1, :]) for f in (0, 1)
    ]
    quantities = [*map(rows_of, source), *faces, *sinks, rows_of(data.coupling)]
    edges = jnp.zeros((1, LANES), F32)
    for q, cells in enumerate(quantities):
        here = (lane1 >= 2 * SIDE * q) & (lane1 < 2 * SIDE * (q + 1))
        edges = jnp.where(here, pltpu.roll(cells, 2 * SIDE * q + SIDE, 1), edges)
    spare = 2 * SIDE * len(quantities)
    edges = jnp.where(lane1 == spare, pltpu.roll(live_first, spare, 1), edges)
    for f in (0, 1):
        before = pltpu.roll(faces[f], spare + 1 + f + SIDE + 1, 1)
        edges = jnp.where(lane1 == spare + 1 + f, before, edges)
    out[pl.ds(2 * CAP, NARROW, stride=UNIT), :] = jnp.where(
        iota((NARROW, LANES), 1) >= LABEL, labels, edges
    )


def interface_level(cells):
    lane = iota(cells.shape, 1)
    spare = 2 * SIDE * 7

    def moved(start, to):
        shift = (to - start) % LANES
        return cells if shift == 0 else pltpu.roll(cells, shift, 1)

    def quantity(q, fill):
        return jnp.where(lane < 2 * SIDE, moved(2 * SIDE * q, 0), fill)

    source = [quantity(0, 0.0), quantity(1, 0.0)]
    live_next = jnp.where(lane == SIDE - 1, moved(spare, SIDE - 1), 1.0)
    faces = [quantity(2, 0.0) * live_next, quantity(3, 0.0) * live_next]
    left = [
        jnp.where(lane == 0, moved(spare + 1 + f, 0), row_prev(faces[f])) for f in (0, 1)
    ]
    sinks = [quantity(4, 1.0), quantity(5, 1.0)]
    return Level(faces, sinks, quantity(6, 0.0), row_prev, row_next, left), source


PARTS = 10


def coarse_level(ref):
    part = load(ref, 5, AGG)
    return Level(part[0:2], part[2:4], part[4], chain_prev, chain_next)


def ready_level(ref, at=0):
    return Level.load(load(ref, PARTS, AGG, at * PARTS * AGG), chain_prev, chain_next)


def store2(ref, v):
    ref[0:AGG, :] = v[0]
    ref[AGG : 2 * AGG, :] = v[1]


def load2(ref):
    return [ref[0:AGG, :], ref[AGG : 2 * AGG, :]]


def coef_kernel(token, face_hbm, sink_hbm, kap_hbm, out, level, face, sink, kap, sems):
    for copy in start_copies((face_hbm, sink_hbm, kap_hbm), (face, sink, kap), sems):
        copy.wait()
    faces, sinks = planar(face, AGG), planar(sink, AGG)
    last = last_cell((AGG, LANES))
    for f in (0, 1):
        out[f * AGG : (f + 1) * AGG, :] = jnp.where(last, 0.0, faces[f])
        out[(2 + f) * AGG : (3 + f) * AGG, :] = sinks[f]
    out[4 * AGG : 5 * AGG, :] = kap[...] * jnp.sqrt(sinks[0] * sinks[1])
    store(level, coarse_level(out).parts())


def pair_kernel(mine, other, out, level):
    out[...] = mine[...] + other[...]
    store(level, coarse_level(out).parts())


def upper_kernel(coef2, coef2_a, coef2_b, coef2_c, levels, near, far, top):
    near[...] = coef2[...] + coef2_a[...]
    far[...] = coef2_b[...] + coef2_c[...]
    top[...] = near[...] + far[...]
    for k, ref in enumerate((near, far, top)):
        store(levels, coarse_level(ref).parts(), k * PARTS * AGG)


def restrict_kernel(narrow, recv, level1, token, leftover, below, drive_out, marks, own_edges):
    n = narrow[0]
    lane = iota((NARROW, LANES), 1)
    src = iota((NARROW, LANES), 0)
    raw = recv[pl.ds(2 * CAP, NARROW, stride=UNIT), :]
    code = jnp.where(lane >= LABEL, raw, 0.0).astype(I32)
    plain = jnp.where(code > 0, (code - 1) % AGG, -1)

    from_end = lane > 2 * SIDE * 7
    for q in range(7):
        from_end = from_end | ((lane >= 2 * SIDE * q) & (lane < 2 * SIDE * q + SIDE))
    cells = jnp.where(from_end, raw, pltpu.roll(raw, NARROW - 1, 0))
    data, source = interface_level(cells)
    field, _ = data.start(source, 2)
    mis = [pltpu.roll(m, LANES - SIDE, 1) for m in data.misfit(field, source)]
    mis = jnp.concatenate(mis, axis=1)
    wide_lane = iota((NARROW, 2 * LANES), 1) % LANES
    real = iota((NARROW, 2 * LANES), 0) < NARROW - 1
    after_end = jnp.where((wide_lane >= LANES - 3) & real, mis, 0.0)
    at_start = jnp.where((wide_lane < 3) & real, mis, 0.0)
    is_end = code > 128
    is_start = (code > 64) & (code <= 128)
    end_at = jnp.max(jnp.where(is_end, plain, -1), axis=1, keepdims=True)
    start_at = jnp.max(jnp.where(is_start, plain, -1), axis=1, keepdims=True)
    end_hot = jnp.where(lane == end_at, 1.0, 0.0)
    start_hot = jnp.where(lane == start_at, 1.0, 0.0)
    start_next = pltpu.roll(start_hot, NARROW - 1, 0)
    zeros = jnp.zeros((2 * NARROW, LANES), F32)
    hot = jnp.transpose(jnp.concatenate([end_hot, start_next, zeros], axis=0), (1, 0))
    edge_hot = hot[0:AGG, :].astype(BF16)
    edge_rows = jnp.concatenate(
        [after_end, at_start, jnp.zeros((2 * NARROW, 2 * LANES), F32)], axis=0
    )

    rows = []
    for t in range(NARROW // 8):
        spread = pltpu.roll(plain[8 * t : 8 * t + 8], CAP, 1, stride=CAP, stride_axis=0)
        mine = jnp.where(lane[0:8] // CAP == src[0:8], spread, 0)
        rows.append(jnp.sum(mine, axis=0, keepdims=True))
    total = select_rows(edge_hot, edge_rows)
    for half in (0, 1):
        hots, parts = [], []
        for t in (2 * half, 2 * half + 1):
            hots.append(iota((AGG, LANES), 0) == rows[t])
            for s in range(8 * t, 8 * t + 8):
                parts.append(
                    jnp.concatenate(
                        [recv[pl.ds(s * UNIT + f, CAP, stride=2), :] for f in (0, 1)], axis=1
                    )
                )
        total = total + select_rows(
            as_bf16(jnp.concatenate(hots, axis=1)), jnp.concatenate(parts, axis=0)
        )
    source_c = [total[:, 0:LANES], total[:, LANES:]]
    level = ready_level(level1)
    correction, drive = level.start(source_c, 2)
    store2(leftover, level.misfit(correction, source_c))
    store2(below, correction)
    store2(drive_out, drive)

    for t in range(NARROW // 8):
        marks[t : t + 1, :] = rows[t].astype(F32)
    marks[8 : 8 + NARROW, :] = pltpu.roll(end_hot, 1, 0)
    marks[8 + NARROW : 8 + 2 * NARROW, :] = start_next
    own_edges[0:1, :] = jnp.sum(jnp.where(src == n - 1, cells, 0.0), axis=0, keepdims=True)
    own_edges[1:2, :] = jnp.sum(jnp.where(src == n, cells, 0.0), axis=0, keepdims=True)


def second_kernel(mine, other, level2, leftover, below, drive_out):
    source = [a + b for a, b in zip(load2(mine), load2(other))]
    level = ready_level(level2)
    correction, drive = level.start(source, 2)
    store2(leftover, level.misfit(correction, source))
    store2(below, correction)
    store2(drive_out, drive)


def side_kernel(marks, own_edges, hot, edges):
    lane = iota((LANES, LANES), 1)
    for t in range(NARROW // 8):
        mark = jnp.broadcast_to(marks[t : t + 1, :], (LANES, LANES))
        mark = jnp.transpose(mark, (1, 0)).astype(I32)
        once = as_bf16(mark == lane % AGG)
        last = as_bf16((mark == lane) & (lane < AGG))
        hot[t * LANES : (t + 1) * LANES, 0:LANES] = once
        hot[t * LANES : (t + 1) * LANES, LANES:] = last
    ends = marks[8 : 8 + 2 * NARROW, :]
    hot[NARROW * CAP :, 0:LANES] = (ends + pltpu.roll(ends, AGG, 1)).astype(BF16)
    hot[NARROW * CAP :, LANES:] = ends.astype(BF16)
    data, source = interface_level(own_edges[...])
    field, drive = data.start(source, 2)
    store(edges, [*field, *drive, *data.parts()[0:7]])


def top_kernel(
    left2, left2_a, left2_b, left2_c, levels, level2, below2, drive2, level1, below1, drive1, hot, out
):
    source3 = [a + b for a, b in zip(load2(left2), load2(left2_a))]
    source3_far = [a + b for a, b in zip(load2(left2_b), load2(left2_c))]
    level3, level3_far, level4 = [ready_level(levels, k) for k in range(3)]
    below3, drive3 = level3.start(source3, 2)
    below3_far, _ = level3_far.start(source3_far, 2)
    source4 = [
        a + b
        for a, b in zip(
            level3.misfit(below3, source3), level3_far.misfit(below3_far, source3_far)
        )
    ]
    v, _ = level4.start(source4, 4)
    v = level3.smooth([a + b for a, b in zip(below3, v)], drive3, 2)
    v = ready_level(level2).smooth([a + b for a, b in zip(load2(below2), v)], load2(drive2), 2)
    v = ready_level(level1).smooth([a + b for a, b in zip(load2(below1), v)], load2(drive1), 2)

    both = jnp.concatenate([v[0], v[1]], axis=1)
    both = jnp.concatenate([*split3(both), jnp.zeros((AGG, 2 * LANES), BF16)], axis=0)
    rows = jnp.dot(hot[...], both, preferred_element_type=F32)
    for s in range(NARROW):
        for f in (0, 1):
            out[pl.ds(s * UNIT + f, CAP, stride=2), :] = rows[
                s * CAP : (s + 1) * CAP, f * LANES : (f + 1) * LANES
            ]
    ends = rows[NARROW * CAP :, :]
    lane = iota((NARROW, LANES), 1)
    halo = []
    for f in (0, 1):
        part = ends[:, f * LANES : (f + 1) * LANES]
        halo.append(jnp.where(lane >= LANES // 2, part[0:NARROW], part[NARROW:]))
    middle = (lane >= LANES // 4) & (lane < LANES * 3 // 4)
    out[pl.ds(2 * CAP, NARROW, stride=UNIT), :] = jnp.where(
        middle, pltpu.roll(halo[1], LANES // 2, 1), halo[0]
    )


def post_kernel(narrow, fine, slots, recv, edges, out):
    n = narrow[0]
    field, drive = load(fine, 2, BLK), load(fine, 2, BLK, 2 * BLK)
    data = Level.load(load(fine, 7, BLK, 4 * BLK), chain_prev, chain_next)
    slot = slots[...].astype(I32)
    lane = iota((BLK, LANES), 1)
    lifted = None
    for half in (0, 1):
        hots, parts = [], []
        for t in (2 * half, 2 * half + 1):
            hots.append(slot == lane + t * LANES)
            for s in range(8 * t, 8 * t + 8):
                parts.append(
                    jnp.concatenate(
                        [recv[pl.ds(s * UNIT + f, CAP, stride=2), :] for f in (0, 1)], axis=1
                    )
                )
        term = select_rows(as_bf16(jnp.concatenate(hots, axis=1)), jnp.concatenate(parts, axis=0))
        lifted = term if lifted is None else lifted + term
    lifted = [lifted[:, 0:LANES], lifted[:, LANES:]]
    v = data.smooth([a + b for a, b in zip(field, lifted)], drive, 2)

    edge_field, edge_drive = load(edges, 2, 8), load(edges, 2, 8, 16)
    edge_data = Level.load(load(edges, 7, 8, 32), row_prev, row_next)
    lane1 = iota((1, LANES), 1)
    row8 = iota((8, LANES), 0)
    edge_v = []
    halo = jnp.sum(recv[pl.ds(2 * CAP, NARROW, stride=UNIT), :], axis=0, keepdims=True)
    for f in (0, 1):
        beyond = halo if f == 0 else pltpu.roll(halo, LANES // 2, 1)
        first = jnp.where(lane1 >= LANES // 2, beyond, lifted[f][0:1, :])
        final = jnp.where(lane1 >= LANES // 2, lifted[f][BLK - 1 : BLK, :], beyond)
        lift = jnp.where(row8 == 0, first, jnp.where(row8 == 1, final, 0.0))
        lift = jnp.where(iota((8, LANES), 1) < 2 * SIDE, pltpu.roll(lift, SIDE, 1), 0.0)
        edge_v.append(edge_field[f] + lift)
    edge_v = edge_data.smooth(edge_v, edge_drive, 2)
    for f in (0, 1):
        out[pl.ds(f, BLK, stride=2), :] = v[f]
        moved = pltpu.roll(edge_v[f], LANES - SIDE, 1)
        out[f : f + 1, :] = jnp.where((lane1 < 4) & (n > 0), moved[0:1, :], v[f][0:1, :])
        final = 2 * (BLK - 1) + f
        out[final : final + 1, :] = jnp.where(
            (lane1 >= LANES - 4) & (n < NARROW - 1), moved[1:2, :], v[f][BLK - 1 : BLK, :]
        )


def call(kernel, outs, *args, spaces=(), scratch=(), cost=None):
    spaces = (*spaces, *[pltpu.VMEM] * (len(args) - len(spaces)))
    args = [
        pltpu.with_memory_space_constraint(a, s) if s == pltpu.HBM else a
        for a, s in zip(args, spaces)
    ]
    return pl.pallas_call(
        kernel,
        out_shape=[jax.ShapeDtypeStruct(s, k) for s, k in outs],
        in_specs=[pl.BlockSpec(memory_space=space) for space in spaces],
        out_specs=[pl.BlockSpec(memory_space=pltpu.VMEM) for _ in outs],
        scratch_shapes=scratch,
        cost_estimate=cost,
        compiler_params=pltpu.CompilerParams(vmem_limit_bytes=32 * 1024 * 1024),
    )(*args)


def exchange(value, bits):
    return lax.ppermute(value, "wide", [(i, i ^ bits) for i in range(lax.axis_size("wide"))])


def to_all(units):
    shape = (NARROW * UNIT, 1, LANES)
    moved = lax.all_to_all(units.reshape(shape), "narrow", 0, 0, tiled=True)
    return moved.reshape(NARROW * UNIT, LANES)


def on_device(
    rhs, fine_face, fine_sink, fine_kap, cell_mask, block_aggregate, coarse_face, coarse_sink, coarse_kap
):
    narrow = lax.axis_index("narrow").astype(I32).reshape(1)
    cells = ((2 * BLK, LANES), F32)
    five, level, two = ((k * AGG, LANES) for k in (5, PARTS, 2))
    five, level, two = (five, F32), (level, F32), (two, F32)
    units = ((NARROW * UNIT, LANES), F32)
    vmem = lambda *rows: [pltpu.VMEM((r, LANES), F32) for r in rows]
    held = vmem(2 * BLK, 2 * BLK, 2 * BLK, BLK) + [pltpu.VMEM((BLK, LANES), I32)]
    beside = pl.CostEstimate(flops=0, bytes_accessed=4 * 1024 * 1024, transcendentals=0)
    fine_args = (
        rhs.reshape(2 * BLK, LANES),
        fine_face.reshape(2 * BLK, LANES),
        fine_sink.reshape(2 * BLK, LANES),
        fine_kap,
        cell_mask,
    )
    sent, slot_row = call(
        pre_kernel,
        [units, ((8, BLK), F32)],
        narrow,
        block_aggregate.reshape(1, BLK),
        *fine_args,
        spaces=(pltpu.SMEM, *[pltpu.HBM] * 6),
        scratch=held + [pltpu.VMEM((1, BLK), I32), pltpu.SemaphoreType.DMA((6,))],
    )
    recv = to_all(sent)
    coef1, level1 = call(
        coef_kernel,
        [five, level],
        slot_row,
        coarse_face.reshape(2 * AGG, LANES),
        coarse_sink.reshape(2 * AGG, LANES),
        coarse_kap,
        spaces=(pltpu.VMEM, *[pltpu.HBM] * 3),
        scratch=vmem(2 * AGG, 2 * AGG, AGG) + [pltpu.SemaphoreType.DMA((3,))],
        cost=beside,
    )
    fine, slots = call(
        ready_kernel,
        [((11 * BLK, LANES), F32), ((BLK, LANES), F32)],
        slot_row,
        *fine_args,
        spaces=(pltpu.VMEM, *[pltpu.HBM] * 5),
        scratch=held + [pltpu.SemaphoreType.DMA((5,))],
        cost=beside,
    )
    coef2, level2 = call(pair_kernel, [five, level], coef1, exchange(coef1, 1), cost=beside)
    (levels,) = call(
        upper_kernel,
        [((3 * PARTS * AGG, LANES), F32)],
        coef2,
        *[exchange(coef2, b) for b in (2, 6, 4)],
        scratch=vmem(5 * AGG, 5 * AGG, 5 * AGG),
        cost=beside,
    )
    left1, below1, drive1, marks, own_edges = call(
        restrict_kernel,
        [two, two, two, ((8 + 2 * NARROW, LANES), F32), ((8, LANES), F32)],
        narrow,
        recv,
        level1,
        fine,
        spaces=(pltpu.SMEM,),
    )
    hot, edges = call(
        side_kernel,
        [((NARROW * CAP + 2 * NARROW, 2 * LANES), BF16), ((11 * 8, LANES), F32)],
        marks,
        own_edges,
    )
    left2, below2, drive2 = call(
        second_kernel, [two, two, two], left1, exchange(left1, 1), level2
    )
    (back,) = call(
        top_kernel,
        [units],
        left2,
        *[exchange(left2, b) for b in (2, 6, 4)],
        levels,
        level2,
        below2,
        drive2,
        level1,
        below1,
        drive1,
        hot,
    )
    recv = to_all(back)
    (out,) = call(post_kernel, [cells], narrow, fine, slots, recv, edges, spaces=(pltpu.SMEM,))
    return out.reshape(BLK, 2, LANES)


def solution(mesh):
    both = ("wide", "narrow")
    placed = (
        P(both, None, None),
        P(both, None, None),
        P(both, None, None),
        P(both, None),
        P(both, None),
        P(both),
        P(both, None, None),
        P(both, None, None),
        P(both, None),
    )
    return jax.shard_map(
        on_device,
        mesh=mesh,
        in_specs=placed,
        out_specs=P(both, None, None),
        check_vma=False,
    )
```

```python
import jax
import jax.numpy as jnp
from jax import lax
from jax.experimental import pallas as pl
from jax.experimental.pallas import tpu as pltpu
from jax.sharding import PartitionSpec as P

OMEGA = 0.8
KEEP = 1.0 - OMEGA
LANES = 128
BLK = 256
AGG = 64
NARROW = 32
CAP = 16
UNIT = 2 * CAP + 1
SIDE = 7
LABEL = LANES - CAP
F32, BF16, I32 = jnp.float32, jnp.bfloat16, jnp.int32


def iota(shape, dim):
    return lax.broadcasted_iota(I32, shape, dim)


def chain_next(v):
    ahead = pltpu.roll(v, LANES - 1, 1)
    below = pltpu.roll(ahead, v.shape[0] - 1, 0)
    return jnp.where(iota(v.shape, 1) == LANES - 1, below, ahead)


def chain_prev(v):
    behind = pltpu.roll(v, 1, 1)
    above = pltpu.roll(behind, 1, 0)
    return jnp.where(iota(v.shape, 1) == 0, above, behind)


def row_next(v):
    return pltpu.roll(v, LANES - 1, 1)


def row_prev(v):
    return pltpu.roll(v, 1, 1)


class Level:
    def __init__(self, faces, sinks, coupling, prev, nxt, left=None):
        self.prev, self.nxt = prev, nxt
        self.faces = faces
        self.left = [prev(f) for f in faces] if left is None else left
        diag = [s + l + f for s, l, f in zip(sinks, self.left, faces)]
        scale = OMEGA / (diag[0] * diag[1] - coupling * coupling)
        self.inv = [diag[1] * scale, diag[0] * scale, coupling * scale]

    def parts(self):
        return [*self.faces, *self.left, *self.inv]

    @classmethod
    def load(cls, part, prev, nxt):
        level = cls.__new__(cls)
        level.prev, level.nxt = prev, nxt
        level.faces, level.left, level.inv = part[0:2], part[2:4], part[4:7]
        return level

    def flow(self, v):
        return [self.left[f] * self.prev(v[f]) + self.faces[f] * self.nxt(v[f]) for f in (0, 1)]

    def step(self, r):
        return [
            self.inv[0] * r[0] + self.inv[2] * r[1],
            self.inv[2] * r[0] + self.inv[1] * r[1],
        ]

    def begin(self, source):
        g = self.step(source)
        w = self.step(self.flow(g))
        field = [(1.0 + KEEP) * a + b for a, b in zip(g, w)]
        return field, [(2.0 * KEEP) * a + b for a, b in zip(g, w)]

    def leftover(self, source, inner):
        return [(KEEP * KEEP) * a + b for a, b in zip(source, self.flow(inner))]

    def again(self, v, field):
        u = self.step(self.flow(v))
        d = self.step(self.flow([(2.0 * KEEP) * a + b for a, b in zip(v, u)]))
        return [(field[f] + (KEEP * KEEP) * v[f]) + d[f] for f in (0, 1)]


def store(ref, parts, at=0):
    for part in parts:
        ref[at : at + part.shape[0], :] = part
        at += part.shape[0]


def load(ref, count, rows, at=0):
    return [ref[at + k * rows : at + (k + 1) * rows, :] for k in range(count)]


def last_cell(shape):
    return (iota(shape, 0) == shape[0] - 1) & (iota(shape, 1) == LANES - 1)


def split3(x):
    hi = x.astype(BF16)
    rest = x - hi.astype(F32)
    mid = rest.astype(BF16)
    return hi, mid, (rest - mid.astype(F32)).astype(BF16)


def select_rows(onehot, x):
    return jnp.dot(
        jnp.concatenate([onehot] * 3, axis=1),
        jnp.concatenate(split3(x), axis=0),
        preferred_element_type=F32,
    )


def as_bf16(mask):
    return jnp.where(mask, 1.0, 0.0).astype(BF16)


def planar(ref, rows):
    return [ref[pl.ds(f, rows, stride=2), :] for f in (0, 1)]


def start_copies(sources, targets, sems):
    copies = [
        pltpu.make_async_copy(a, b, sems.at[k]) for k, (a, b) in enumerate(zip(sources, targets))
    ]
    for copy in copies:
        copy.start()
    return copies


def fine_start(rhs, face, sink, kap, mask):
    live = mask[...].astype(F32)
    live_next = jnp.where(last_cell((BLK, LANES)), 0.0, chain_next(live))
    both = live * live_next
    sinks = planar(sink, BLK)
    coupling = kap[...] * jnp.sqrt(sinks[0] * sinks[1]) * live
    data = Level([f * both for f in planar(face, BLK)], sinks, coupling, chain_prev, chain_next)
    source = [r * live for r in planar(rhs, BLK)]
    return data, coupling, source, *data.begin(source)


def ready_kernel(slot_row, *refs):
    inputs, fine, slots, held, sems = refs[0:5], refs[5], refs[6], refs[7:12], refs[12]
    copies = start_copies(inputs, held, sems)
    slots[...] = jnp.transpose(jnp.broadcast_to(slot_row[0:1, :], (LANES, BLK)), (1, 0))
    for copy in copies:
        copy.wait()
    data, _, _, field, _ = fine_start(*held)
    store(fine, [*field, *data.parts()])


def pre_kernel(narrow, agg_hbm, *refs):
    inputs, out, slots, held, sems = refs[0:5], refs[5], refs[6], refs[7:13], refs[13]
    rhs, face, sink, kap, mask, agg = held
    n = narrow[0]
    for copy in start_copies((*inputs, agg_hbm), held, sems):
        copy.wait()

    label = agg[...]
    owner = label // AGG
    within = label - owner * AGG
    owned = iota((NARROW, BLK), 0) == owner
    before = as_bf16(iota((BLK, BLK), 0) < iota((BLK, BLK), 1))
    counts = jnp.dot(as_bf16(owned), before, preferred_element_type=F32)
    rank = jnp.sum(jnp.where(owned, counts, 0.0), axis=0, keepdims=True).astype(I32)
    slot = owner * CAP + rank
    put = as_bf16(iota((NARROW * CAP, BLK), 0) == slot)

    block = iota((1, BLK), 1)
    code = within + 1 + jnp.where(block == 0, 64, 0) + jnp.where(block == BLK - 1, 128, 0)
    coded = jnp.where(owned, code.astype(F32), 0.0).astype(BF16)
    at_rank = as_bf16(iota((LANES, BLK), 0) % CAP == rank)
    labels = lax.dot_general(
        coded, at_rank, (((1,), (1,)), ((), ())), preferred_element_type=F32
    )
    slots[...] = jnp.broadcast_to(slot.astype(F32), (8, BLK))

    data, coupling, source, _, inner = fine_start(rhs, face, sink, kap, mask)
    misfit = data.leftover(source, inner)
    row, lane = iota((BLK, LANES), 0), iota((BLK, LANES), 1)
    drop = ((row == BLK - 1) & (lane >= LANES - 3) & (n < NARROW - 1)) | (
        (row == 0) & (lane < 3) & (n > 0)
    )
    misfit = jnp.concatenate([jnp.where(drop, 0.0, m) for m in misfit], axis=1)

    rows = select_rows(put, misfit)
    for o in range(NARROW):
        for f in (0, 1):
            out[pl.ds(o * UNIT + f, CAP, stride=2), :] = rows[
                o * CAP : (o + 1) * CAP, f * LANES : (f + 1) * LANES
            ]

    lane1 = iota((1, LANES), 1)

    def ends(final, first):
        return jnp.where(lane1 >= LANES // 2, final, first)

    def rows_of(v):
        return ends(v[BLK - 1 : BLK, :], v[0:1, :])

    live_first = mask[0:1, :].astype(F32)
    live_final = mask[BLK - 1 : BLK, :].astype(F32)
    faces = []
    for f in (0, 1):
        open_face = face[2 * (BLK - 1) + f : 2 * (BLK - 1) + f + 1, :] * live_final
        final = jnp.where(lane1 == LANES - 1, open_face, data.faces[f][BLK - 1 : BLK, :])
        faces.append(ends(final, data.faces[f][0:1, :]))
    sinks = [
        ends(sink[2 * (BLK - 1) + f : 2 * (BLK - 1) + f + 1, :], sink[f : f + 1, :]) for f in (0, 1)
    ]
    quantities = [*map(rows_of, source), *faces, *sinks, rows_of(coupling)]
    edges = jnp.zeros((1, LANES), F32)
    for q, cells in enumerate(quantities):
        here = (lane1 >= 2 * SIDE * q) & (lane1 < 2 * SIDE * (q + 1))
        edges = jnp.where(here, pltpu.roll(cells, 2 * SIDE * q + SIDE, 1), edges)
    spare = 2 * SIDE * len(quantities)
    edges = jnp.where(lane1 == spare, pltpu.roll(live_first, spare, 1), edges)
    for f in (0, 1):
        before = pltpu.roll(faces[f], spare + 1 + f + SIDE + 1, 1)
        edges = jnp.where(lane1 == spare + 1 + f, before, edges)
    out[pl.ds(2 * CAP, NARROW, stride=UNIT), :] = jnp.where(
        iota((NARROW, LANES), 1) >= LABEL, labels, edges
    )


def interface_level(cells):
    lane = iota(cells.shape, 1)
    spare = 2 * SIDE * 7

    def moved(start, to):
        shift = (to - start) % LANES
        return cells if shift == 0 else pltpu.roll(cells, shift, 1)

    def quantity(q, fill):
        return jnp.where(lane < 2 * SIDE, moved(2 * SIDE * q, 0), fill)

    source = [quantity(0, 0.0), quantity(1, 0.0)]
    live_next = jnp.where(lane == SIDE - 1, moved(spare, SIDE - 1), 1.0)
    faces = [quantity(2, 0.0) * live_next, quantity(3, 0.0) * live_next]
    left = [
        jnp.where(lane == 0, moved(spare + 1 + f, 0), row_prev(faces[f])) for f in (0, 1)
    ]
    sinks = [quantity(4, 1.0), quantity(5, 1.0)]
    return Level(faces, sinks, quantity(6, 0.0), row_prev, row_next, left), source


PARTS = 7
REACH = (2, 1, 0, -1, -2)
TWICE = 4 * len(REACH)
LEVEL_ROWS = (PARTS + TWICE) * AGG


def shifted(v, cells):
    if cells == 0:
        return v
    moved = pltpu.roll(v, cells % LANES, 1)
    lane = iota(v.shape, 1)
    if cells > 0:
        return jnp.where(lane < cells, pltpu.roll(moved, 1, 0), moved)
    return jnp.where(lane >= LANES + cells, pltpu.roll(moved, v.shape[0] - 1, 0), moved)


def product(a, b):
    return [
        a[0] * b[0] + a[1] * b[2],
        a[0] * b[1] + a[1] * b[3],
        a[2] * b[0] + a[3] * b[2],
        a[2] * b[1] + a[3] * b[3],
    ]


def plus(a, b):
    return [x + y for x, y in zip(a, b)]


def apply_blocks(blocks, v):
    total = [None, None]
    terms = [[], []]
    for k, cells in enumerate(REACH):
        block, at = blocks[4 * k : 4 * k + 4], [shifted(x, cells) for x in v]
        for f in (0, 1):
            terms[f].append(block[2 * f] * at[0] + block[2 * f + 1] * at[1])
    for f in (0, 1):
        a, b, c, d, e = terms[f]
        total[f] = c + ((a + b) + (d + e))
    return total


class Coarse:
    @staticmethod
    def build(coef, out, at=0, again=True):
        part = load(coef, 5, AGG)
        level = Level(part[0:2], part[2:4], part[4], chain_prev, chain_next)
        store(out, level.parts(), at * LEVEL_ROWS)
        if not again:
            return
        (l0, l1), (r0, r1), (i0, i1, i2) = level.left, level.faces, level.inv
        from_left = [i0 * l0, i2 * l1, i2 * l0, i1 * l1]
        from_right = [i0 * r0, i2 * r1, i2 * r0, i1 * r1]
        left_before, right_before = ([chain_prev(x) for x in b] for b in (from_left, from_right))
        left_after, right_after = ([chain_next(x) for x in b] for b in (from_left, from_right))
        keep = jnp.full_like(l0, KEEP * KEEP)
        zero = jnp.zeros_like(l0)
        double = 2.0 * KEEP
        twice = [
            *product(from_left, left_before),
            *[double * x for x in from_left],
            *plus(
                [keep, zero, zero, keep],
                plus(product(from_left, right_before), product(from_right, left_after)),
            ),
            *[double * x for x in from_right],
            *product(from_right, right_after),
        ]
        store(out, twice, at * LEVEL_ROWS + PARTS * AGG)

    def __init__(self, ref, at=0):
        self.ref, self.at = ref, at * LEVEL_ROWS
        self.level = Level.load(load(ref, PARTS, AGG, self.at), chain_prev, chain_next)

    def begin(self, source):
        field, inner = self.level.begin(source)
        return field, self.level.leftover(source, inner)

    def again(self, v, field):
        return plus(field, apply_blocks(load(self.ref, TWICE, AGG, self.at + PARTS * AGG), v))


def store2(ref, v):
    ref[0:AGG, :] = v[0]
    ref[AGG : 2 * AGG, :] = v[1]


def load2(ref):
    return [ref[0:AGG, :], ref[AGG : 2 * AGG, :]]


def coef_kernel(token, face_hbm, sink_hbm, kap_hbm, out, level, face, sink, kap, sems):
    for copy in start_copies((face_hbm, sink_hbm, kap_hbm), (face, sink, kap), sems):
        copy.wait()
    faces, sinks = planar(face, AGG), planar(sink, AGG)
    last = last_cell((AGG, LANES))
    for f in (0, 1):
        out[f * AGG : (f + 1) * AGG, :] = jnp.where(last, 0.0, faces[f])
        out[(2 + f) * AGG : (3 + f) * AGG, :] = sinks[f]
    out[4 * AGG : 5 * AGG, :] = kap[...] * jnp.sqrt(sinks[0] * sinks[1])
    Coarse.build(out, level)


def pair_kernel(mine, other, out, level):
    out[...] = mine[...] + other[...]
    Coarse.build(out, level)


def upper_kernel(coef2, coef2_a, coef2_b, coef2_c, levels, near, far, top):
    near[...] = coef2[...] + coef2_a[...]
    far[...] = coef2_b[...] + coef2_c[...]
    top[...] = near[...] + far[...]
    for k, ref in enumerate((near, top, far)):
        Coarse.build(ref, levels, k, ref is not far)


def restrict_kernel(narrow, recv, level1, token, leftover, below, marks, own_edges):
    n = narrow[0]
    lane = iota((NARROW, LANES), 1)
    src = iota((NARROW, LANES), 0)
    raw = recv[pl.ds(2 * CAP, NARROW, stride=UNIT), :]
    code = jnp.where(lane >= LABEL, raw, 0.0).astype(I32)
    plain = jnp.where(code > 0, (code - 1) % AGG, -1)

    from_end = lane > 2 * SIDE * 7
    for q in range(7):
        from_end = from_end | ((lane >= 2 * SIDE * q) & (lane < 2 * SIDE * q + SIDE))
    cells = jnp.where(from_end, raw, pltpu.roll(raw, NARROW - 1, 0))
    data, source = interface_level(cells)
    _, inner = data.begin(source)
    mis = [pltpu.roll(m, LANES - SIDE, 1) for m in data.leftover(source, inner)]
    mis = jnp.concatenate(mis, axis=1)
    wide_lane = iota((NARROW, 2 * LANES), 1) % LANES
    real = iota((NARROW, 2 * LANES), 0) < NARROW - 1
    after_end = jnp.where((wide_lane >= LANES - 3) & real, mis, 0.0)
    at_start = jnp.where((wide_lane < 3) & real, mis, 0.0)
    is_end = code > 128
    is_start = (code > 64) & (code <= 128)
    end_at = jnp.max(jnp.where(is_end, plain, -1), axis=1, keepdims=True)
    start_at = jnp.max(jnp.where(is_start, plain, -1), axis=1, keepdims=True)
    end_hot = jnp.where(lane == end_at, 1.0, 0.0)
    start_hot = jnp.where(lane == start_at, 1.0, 0.0)
    start_next = pltpu.roll(start_hot, NARROW - 1, 0)
    zeros = jnp.zeros((2 * NARROW, LANES), F32)
    hot = jnp.transpose(jnp.concatenate([end_hot, start_next, zeros], axis=0), (1, 0))
    edge_hot = hot[0:AGG, :].astype(BF16)
    edge_rows = jnp.concatenate(
        [after_end, at_start, jnp.zeros((2 * NARROW, 2 * LANES), F32)], axis=0
    )

    rows = []
    for t in range(NARROW // 8):
        spread = pltpu.roll(plain[8 * t : 8 * t + 8], CAP, 1, stride=CAP, stride_axis=0)
        mine = jnp.where(lane[0:8] // CAP == src[0:8], spread, 0)
        rows.append(jnp.sum(mine, axis=0, keepdims=True))
    total = select_rows(edge_hot, edge_rows)
    for half in (0, 1):
        hots, parts = [], []
        for t in (2 * half, 2 * half + 1):
            hots.append(iota((AGG, LANES), 0) == rows[t])
            for s in range(8 * t, 8 * t + 8):
                parts.append(
                    jnp.concatenate(
                        [recv[pl.ds(s * UNIT + f, CAP, stride=2), :] for f in (0, 1)], axis=1
                    )
                )
        total = total + select_rows(
            as_bf16(jnp.concatenate(hots, axis=1)), jnp.concatenate(parts, axis=0)
        )
    source_c = [total[:, 0:LANES], total[:, LANES:]]
    correction, rest = Coarse(level1).begin(source_c)
    store2(leftover, rest)
    store2(below, correction)

    for t in range(NARROW // 8):
        marks[t : t + 1, :] = rows[t].astype(F32)
    marks[8 : 8 + NARROW, :] = pltpu.roll(end_hot, 1, 0)
    marks[8 + NARROW : 8 + 2 * NARROW, :] = start_next
    own_edges[0:1, :] = jnp.sum(jnp.where(src == n - 1, cells, 0.0), axis=0, keepdims=True)
    own_edges[1:2, :] = jnp.sum(jnp.where(src == n, cells, 0.0), axis=0, keepdims=True)


def second_kernel(mine, other, level2, leftover, below):
    source = [a + b for a, b in zip(load2(mine), load2(other))]
    correction, rest = Coarse(level2).begin(source)
    store2(leftover, rest)
    store2(below, correction)


def side_kernel(marks, own_edges, hot, edges):
    lane = iota((LANES, LANES), 1)
    for t in range(NARROW // 8):
        mark = jnp.broadcast_to(marks[t : t + 1, :], (LANES, LANES))
        mark = jnp.transpose(mark, (1, 0)).astype(I32)
        once = as_bf16(mark == lane % AGG)
        last = as_bf16((mark == lane) & (lane < AGG))
        hot[t * LANES : (t + 1) * LANES, 0:LANES] = once
        hot[t * LANES : (t + 1) * LANES, LANES:] = last
    ends = marks[8 : 8 + 2 * NARROW, :]
    hot[NARROW * CAP :, 0:LANES] = (ends + pltpu.roll(ends, AGG, 1)).astype(BF16)
    hot[NARROW * CAP :, LANES:] = ends.astype(BF16)
    data, source = interface_level(own_edges[...])
    field, _ = data.begin(source)
    store(edges, [*field, *data.parts()])


def top_kernel(
    left2, left2_a, left2_b, left2_c, levels, level2, below2, level1, below1, hot, out
):
    source3 = [a + b for a, b in zip(load2(left2), load2(left2_a))]
    source3_far = [a + b for a, b in zip(load2(left2_b), load2(left2_c))]
    level3, level4, level3_far = [Coarse(levels, k) for k in range(3)]
    below3, rest = level3.begin(source3)
    _, rest_far = level3_far.begin(source3_far)
    v, _ = level4.begin(plus(rest, rest_far))
    v = level4.again(v, v)
    for level, field in (
        (level3, below3),
        (Coarse(level2), load2(below2)),
        (Coarse(level1), load2(below1)),
    ):
        v = level.again(plus(field, v), field)

    both = jnp.concatenate([v[0], v[1]], axis=1)
    both = jnp.concatenate([*split3(both), jnp.zeros((AGG, 2 * LANES), BF16)], axis=0)
    rows = jnp.dot(hot[...], both, preferred_element_type=F32)
    for s in range(NARROW):
        for f in (0, 1):
            out[pl.ds(s * UNIT + f, CAP, stride=2), :] = rows[
                s * CAP : (s + 1) * CAP, f * LANES : (f + 1) * LANES
            ]
    ends = rows[NARROW * CAP :, :]
    lane = iota((NARROW, LANES), 1)
    halo = []
    for f in (0, 1):
        part = ends[:, f * LANES : (f + 1) * LANES]
        halo.append(jnp.where(lane >= LANES // 2, part[0:NARROW], part[NARROW:]))
    middle = (lane >= LANES // 4) & (lane < LANES * 3 // 4)
    out[pl.ds(2 * CAP, NARROW, stride=UNIT), :] = jnp.where(
        middle, pltpu.roll(halo[1], LANES // 2, 1), halo[0]
    )


def post_kernel(narrow, fine, slots, recv, edges, out):
    n = narrow[0]
    field = load(fine, 2, BLK)
    data = Level.load(load(fine, PARTS, BLK, 2 * BLK), chain_prev, chain_next)
    slot = slots[...].astype(I32)
    lane = iota((BLK, LANES), 1)
    lifted = None
    for half in (0, 1):
        hots, parts = [], []
        for t in (2 * half, 2 * half + 1):
            hots.append(slot == lane + t * LANES)
            for s in range(8 * t, 8 * t + 8):
                parts.append(
                    jnp.concatenate(
                        [recv[pl.ds(s * UNIT + f, CAP, stride=2), :] for f in (0, 1)], axis=1
                    )
                )
        term = select_rows(as_bf16(jnp.concatenate(hots, axis=1)), jnp.concatenate(parts, axis=0))
        lifted = term if lifted is None else lifted + term
    lifted = [lifted[:, 0:LANES], lifted[:, LANES:]]
    v = data.again([a + b for a, b in zip(field, lifted)], field)

    edge_field = load(edges, 2, 8)
    edge_data = Level.load(load(edges, PARTS, 8, 16), row_prev, row_next)
    lane1 = iota((1, LANES), 1)
    row8 = iota((8, LANES), 0)
    edge_v = []
    halo = jnp.sum(recv[pl.ds(2 * CAP, NARROW, stride=UNIT), :], axis=0, keepdims=True)
    for f in (0, 1):
        beyond = halo if f == 0 else pltpu.roll(halo, LANES // 2, 1)
        first = jnp.where(lane1 >= LANES // 2, beyond, lifted[f][0:1, :])
        final = jnp.where(lane1 >= LANES // 2, lifted[f][BLK - 1 : BLK, :], beyond)
        lift = jnp.where(row8 == 0, first, jnp.where(row8 == 1, final, 0.0))
        lift = jnp.where(iota((8, LANES), 1) < 2 * SIDE, pltpu.roll(lift, SIDE, 1), 0.0)
        edge_v.append(edge_field[f] + lift)
    edge_v = edge_data.again(edge_v, edge_field)
    for f in (0, 1):
        out[pl.ds(f, BLK, stride=2), :] = v[f]
        moved = pltpu.roll(edge_v[f], LANES - SIDE, 1)
        out[f : f + 1, :] = jnp.where((lane1 < 4) & (n > 0), moved[0:1, :], v[f][0:1, :])
        final = 2 * (BLK - 1) + f
        out[final : final + 1, :] = jnp.where(
            (lane1 >= LANES - 4) & (n < NARROW - 1), moved[1:2, :], v[f][BLK - 1 : BLK, :]
        )


def call(kernel, outs, *args, spaces=(), scratch=(), cost=None):
    spaces = (*spaces, *[pltpu.VMEM] * (len(args) - len(spaces)))
    args = [
        pltpu.with_memory_space_constraint(a, s) if s == pltpu.HBM else a
        for a, s in zip(args, spaces)
    ]
    return pl.pallas_call(
        kernel,
        out_shape=[jax.ShapeDtypeStruct(s, k) for s, k in outs],
        in_specs=[pl.BlockSpec(memory_space=space) for space in spaces],
        out_specs=[pl.BlockSpec(memory_space=pltpu.VMEM) for _ in outs],
        scratch_shapes=scratch,
        cost_estimate=cost,
        compiler_params=pltpu.CompilerParams(vmem_limit_bytes=32 * 1024 * 1024),
    )(*args)


def exchange(value, bits):
    return lax.ppermute(value, "wide", [(i, i ^ bits) for i in range(lax.axis_size("wide"))])


def to_all(units):
    shape = (NARROW * UNIT, 1, LANES)
    moved = lax.all_to_all(units.reshape(shape), "narrow", 0, 0, tiled=True)
    return moved.reshape(NARROW * UNIT, LANES)


def on_device(
    rhs, fine_face, fine_sink, fine_kap, cell_mask, block_aggregate, coarse_face, coarse_sink, coarse_kap
):
    narrow = lax.axis_index("narrow").astype(I32).reshape(1)
    cells = ((2 * BLK, LANES), F32)
    five, level, two = (5 * AGG, LANES), (LEVEL_ROWS, LANES), (2 * AGG, LANES)
    five, level, two = (five, F32), (level, F32), (two, F32)
    units = ((NARROW * UNIT, LANES), F32)
    vmem = lambda *rows: [pltpu.VMEM((r, LANES), F32) for r in rows]
    held = vmem(2 * BLK, 2 * BLK, 2 * BLK, BLK) + [pltpu.VMEM((BLK, LANES), I32)]
    beside = pl.CostEstimate(flops=0, bytes_accessed=4 * 1024 * 1024, transcendentals=0)
    fine_args = (
        rhs.reshape(2 * BLK, LANES),
        fine_face.reshape(2 * BLK, LANES),
        fine_sink.reshape(2 * BLK, LANES),
        fine_kap,
        cell_mask,
    )
    sent, slot_row = call(
        pre_kernel,
        [units, ((8, BLK), F32)],
        narrow,
        block_aggregate.reshape(1, BLK),
        *fine_args,
        spaces=(pltpu.SMEM, *[pltpu.HBM] * 6),
        scratch=held + [pltpu.VMEM((1, BLK), I32), pltpu.SemaphoreType.DMA((6,))],
    )
    recv = to_all(sent)
    coef1, level1 = call(
        coef_kernel,
        [five, level],
        slot_row,
        coarse_face.reshape(2 * AGG, LANES),
        coarse_sink.reshape(2 * AGG, LANES),
        coarse_kap,
        spaces=(pltpu.VMEM, *[pltpu.HBM] * 3),
        scratch=vmem(2 * AGG, 2 * AGG, AGG) + [pltpu.SemaphoreType.DMA((3,))],
        cost=beside,
    )
    fine, slots = call(
        ready_kernel,
        [((9 * BLK, LANES), F32), ((BLK, LANES), F32)],
        slot_row,
        *fine_args,
        spaces=(pltpu.VMEM, *[pltpu.HBM] * 5),
        scratch=held + [pltpu.SemaphoreType.DMA((5,))],
        cost=beside,
    )
    coef2, level2 = call(pair_kernel, [five, level], coef1, exchange(coef1, 1), cost=beside)
    (levels,) = call(
        upper_kernel,
        [((2 * LEVEL_ROWS + PARTS * AGG, LANES), F32)],
        coef2,
        *[exchange(coef2, b) for b in (2, 6, 4)],
        scratch=vmem(5 * AGG, 5 * AGG, 5 * AGG),
        cost=beside,
    )
    left1, below1, marks, own_edges = call(
        restrict_kernel,
        [two, two, ((8 + 2 * NARROW, LANES), F32), ((8, LANES), F32)],
        narrow,
        recv,
        level1,
        fine,
        spaces=(pltpu.SMEM,),
    )
    hot, edges = call(
        side_kernel,
        [((NARROW * CAP + 2 * NARROW, 2 * LANES), BF16), ((9 * 8, LANES), F32)],
        marks,
        own_edges,
    )
    left2, below2 = call(
        second_kernel, [two, two], left1, exchange(left1, 1), level2
    )
    (back,) = call(
        top_kernel,
        [units],
        left2,
        *[exchange(left2, b) for b in (2, 6, 4)],
        levels,
        level2,
        below2,
        level1,
        below1,
        hot,
    )
    recv = to_all(back)
    (out,) = call(post_kernel, [cells], narrow, fine, slots, recv, edges, spaces=(pltpu.SMEM,))
    return out.reshape(BLK, 2, LANES)


def solution(mesh):
    both = ("wide", "narrow")
    placed = (
        P(both, None, None),
        P(both, None, None),
        P(both, None, None),
        P(both, None),
        P(both, None),
        P(both),
        P(both, None, None),
        P(both, None, None),
        P(both, None),
    )
    return jax.shard_map(
        on_device,
        mesh=mesh,
        in_specs=placed,
        out_specs=P(both, None, None),
        check_vma=False,
    )
```

```python
import jax
import jax.numpy as jnp
from jax import lax
from jax.experimental import pallas as pl
from jax.experimental.pallas import tpu as pltpu
from jax.sharding import PartitionSpec as P

OMEGA = 0.8
KEEP = 1.0 - OMEGA
LANES = 128
BLK = 256
AGG = 64
NARROW = 32
CAP = 16
UNIT = 2 * CAP + 1
SIDE = 7
LABEL = LANES - CAP
F32, BF16, I32 = jnp.float32, jnp.bfloat16, jnp.int32


def iota(shape, dim):
    return lax.broadcasted_iota(I32, shape, dim)


def chain_next(v):
    ahead = pltpu.roll(v, LANES - 1, 1)
    below = pltpu.roll(ahead, v.shape[0] - 1, 0)
    return jnp.where(iota(v.shape, 1) == LANES - 1, below, ahead)


def chain_prev(v):
    behind = pltpu.roll(v, 1, 1)
    above = pltpu.roll(behind, 1, 0)
    return jnp.where(iota(v.shape, 1) == 0, above, behind)


def row_next(v):
    return pltpu.roll(v, LANES - 1, 1)


def row_prev(v):
    return pltpu.roll(v, 1, 1)


class Level:
    def __init__(self, faces, sinks, coupling, prev, nxt, left=None):
        self.prev, self.nxt = prev, nxt
        self.faces = faces
        self.left = [prev(f) for f in faces] if left is None else left
        diag = [s + l + f for s, l, f in zip(sinks, self.left, faces)]
        scale = OMEGA / (diag[0] * diag[1] - coupling * coupling)
        self.inv = [diag[1] * scale, diag[0] * scale, coupling * scale]

    def parts(self):
        return [*self.faces, *self.left, *self.inv]

    @classmethod
    def load(cls, part, prev, nxt):
        level = cls.__new__(cls)
        level.prev, level.nxt = prev, nxt
        level.faces, level.left, level.inv = part[0:2], part[2:4], part[4:7]
        return level

    def flow(self, v):
        return [self.left[f] * self.prev(v[f]) + self.faces[f] * self.nxt(v[f]) for f in (0, 1)]

    def step(self, r):
        return [
            self.inv[0] * r[0] + self.inv[2] * r[1],
            self.inv[2] * r[0] + self.inv[1] * r[1],
        ]

    def begin(self, source):
        g = self.step(source)
        w = self.step(self.flow(g))
        field = [(1.0 + KEEP) * a + b for a, b in zip(g, w)]
        return field, [(2.0 * KEEP) * a + b for a, b in zip(g, w)]

    def leftover(self, source, inner):
        return [(KEEP * KEEP) * a + b for a, b in zip(source, self.flow(inner))]

    def again(self, v, field):
        u = self.step(self.flow(v))
        d = self.step(self.flow([(2.0 * KEEP) * a + b for a, b in zip(v, u)]))
        return [(field[f] + (KEEP * KEEP) * v[f]) + d[f] for f in (0, 1)]


def store(ref, parts, at=0):
    for part in parts:
        ref[at : at + part.shape[0], :] = part
        at += part.shape[0]


def load(ref, count, rows, at=0):
    return [ref[at + k * rows : at + (k + 1) * rows, :] for k in range(count)]


def last_cell(shape):
    return (iota(shape, 0) == shape[0] - 1) & (iota(shape, 1) == LANES - 1)


def split3(x):
    hi = x.astype(BF16)
    rest = x - hi.astype(F32)
    mid = rest.astype(BF16)
    return hi, mid, (rest - mid.astype(F32)).astype(BF16)


def select_rows(onehot, x):
    return jnp.dot(
        jnp.concatenate([onehot] * 3, axis=1),
        jnp.concatenate(split3(x), axis=0),
        preferred_element_type=F32,
    )


def as_bf16(mask):
    return jnp.where(mask, 1.0, 0.0).astype(BF16)


def planar(ref, rows):
    return [ref[pl.ds(f, rows, stride=2), :] for f in (0, 1)]


def start_copies(sources, targets, sems):
    copies = [
        pltpu.make_async_copy(a, b, sems.at[k]) for k, (a, b) in enumerate(zip(sources, targets))
    ]
    for copy in copies:
        copy.start()
    return copies


def fine_start(rhs, face, sink, kap, mask):
    live = mask[...].astype(F32)
    live_next = jnp.where(last_cell((BLK, LANES)), 0.0, chain_next(live))
    both = live * live_next
    sinks = planar(sink, BLK)
    coupling = kap[...] * jnp.sqrt(sinks[0] * sinks[1]) * live
    data = Level([f * both for f in planar(face, BLK)], sinks, coupling, chain_prev, chain_next)
    source = [r * live for r in planar(rhs, BLK)]
    return data, coupling, source, *data.begin(source)


def ready_kernel(slot_row, *refs):
    inputs, fine, slots, held, sems = refs[0:5], refs[5], refs[6], refs[7:12], refs[12]
    copies = start_copies(inputs, held, sems)
    slots[...] = jnp.transpose(jnp.broadcast_to(slot_row[0:1, :], (LANES, BLK)), (1, 0))
    for copy in copies:
        copy.wait()
    data, _, _, field, _ = fine_start(*held)
    store(fine, [*field, *data.parts()])


def pre_kernel(narrow, agg_hbm, *refs):
    inputs, out, slots, held, sems = refs[0:5], refs[5], refs[6], refs[7:13], refs[13]
    rhs, face, sink, kap, mask, agg = held
    n = narrow[0]
    for copy in start_copies((*inputs, agg_hbm), held, sems):
        copy.wait()

    label = agg[...]
    owner = label // AGG
    within = label - owner * AGG
    owned = iota((NARROW, BLK), 0) == owner
    before = as_bf16(iota((BLK, BLK), 0) < iota((BLK, BLK), 1))
    counts = jnp.dot(as_bf16(owned), before, preferred_element_type=F32)
    rank = jnp.sum(jnp.where(owned, counts, 0.0), axis=0, keepdims=True).astype(I32)
    slot = owner * CAP + rank
    put = as_bf16(iota((NARROW * CAP, BLK), 0) == slot)

    block = iota((1, BLK), 1)
    code = within + 1 + jnp.where(block == 0, 64, 0) + jnp.where(block == BLK - 1, 128, 0)
    coded = jnp.where(owned, code.astype(F32), 0.0).astype(BF16)
    at_rank = as_bf16(iota((LANES, BLK), 0) % CAP == rank)
    labels = lax.dot_general(
        coded, at_rank, (((1,), (1,)), ((), ())), preferred_element_type=F32
    )
    slots[...] = jnp.broadcast_to(slot.astype(F32), (8, BLK))

    data, coupling, source, _, inner = fine_start(rhs, face, sink, kap, mask)
    misfit = data.leftover(source, inner)
    row, lane = iota((BLK, LANES), 0), iota((BLK, LANES), 1)
    drop = ((row == BLK - 1) & (lane >= LANES - 3) & (n < NARROW - 1)) | (
        (row == 0) & (lane < 3) & (n > 0)
    )
    misfit = jnp.concatenate([jnp.where(drop, 0.0, m) for m in misfit], axis=1)

    rows = select_rows(put, misfit)
    for o in range(NARROW):
        for f in (0, 1):
            out[pl.ds(o * UNIT + f, CAP, stride=2), :] = rows[
                o * CAP : (o + 1) * CAP, f * LANES : (f + 1) * LANES
            ]

    lane1 = iota((1, LANES), 1)

    def ends(final, first):
        return jnp.where(lane1 >= LANES // 2, final, first)

    def rows_of(v):
        return ends(v[BLK - 1 : BLK, :], v[0:1, :])

    live_first = mask[0:1, :].astype(F32)
    live_final = mask[BLK - 1 : BLK, :].astype(F32)
    faces = []
    for f in (0, 1):
        open_face = face[2 * (BLK - 1) + f : 2 * (BLK - 1) + f + 1, :] * live_final
        final = jnp.where(lane1 == LANES - 1, open_face, data.faces[f][BLK - 1 : BLK, :])
        faces.append(ends(final, data.faces[f][0:1, :]))
    sinks = [
        ends(sink[2 * (BLK - 1) + f : 2 * (BLK - 1) + f + 1, :], sink[f : f + 1, :]) for f in (0, 1)
    ]
    quantities = [*map(rows_of, source), *faces, *sinks, rows_of(coupling)]
    edges = jnp.zeros((1, LANES), F32)
    for q, cells in enumerate(quantities):
        here = (lane1 >= 2 * SIDE * q) & (lane1 < 2 * SIDE * (q + 1))
        edges = jnp.where(here, pltpu.roll(cells, 2 * SIDE * q + SIDE, 1), edges)
    spare = 2 * SIDE * len(quantities)
    edges = jnp.where(lane1 == spare, pltpu.roll(live_first, spare, 1), edges)
    for f in (0, 1):
        before = pltpu.roll(faces[f], spare + 1 + f + SIDE + 1, 1)
        edges = jnp.where(lane1 == spare + 1 + f, before, edges)
    out[pl.ds(2 * CAP, NARROW, stride=UNIT), :] = jnp.where(
        iota((NARROW, LANES), 1) >= LABEL, labels, edges
    )


def interface_level(cells):
    lane = iota(cells.shape, 1)
    spare = 2 * SIDE * 7

    def moved(start, to):
        shift = (to - start) % LANES
        return cells if shift == 0 else pltpu.roll(cells, shift, 1)

    def quantity(q, fill):
        return jnp.where(lane < 2 * SIDE, moved(2 * SIDE * q, 0), fill)

    source = [quantity(0, 0.0), quantity(1, 0.0)]
    live_next = jnp.where(lane == SIDE - 1, moved(spare, SIDE - 1), 1.0)
    faces = [quantity(2, 0.0) * live_next, quantity(3, 0.0) * live_next]
    left = [
        jnp.where(lane == 0, moved(spare + 1 + f, 0), row_prev(faces[f])) for f in (0, 1)
    ]
    sinks = [quantity(4, 1.0), quantity(5, 1.0)]
    return Level(faces, sinks, quantity(6, 0.0), row_prev, row_next, left), source


PARTS = 7
REACH = (2, 0, -2)
TWICE = 4 * len(REACH)
LEVEL_ROWS = (PARTS + TWICE) * AGG


def shifted(v, cells):
    if cells == 0:
        return v
    moved = pltpu.roll(v, cells % LANES, 1)
    lane = iota(v.shape, 1)
    if cells > 0:
        return jnp.where(lane < cells, pltpu.roll(moved, 1, 0), moved)
    return jnp.where(lane >= LANES + cells, pltpu.roll(moved, v.shape[0] - 1, 0), moved)


def product(a, b):
    return [
        a[0] * b[0] + a[1] * b[2],
        a[0] * b[1] + a[1] * b[3],
        a[2] * b[0] + a[3] * b[2],
        a[2] * b[1] + a[3] * b[3],
    ]


def plus(a, b):
    return [x + y for x, y in zip(a, b)]


def apply_blocks(blocks, v):
    terms = []
    for k, cells in enumerate(REACH):
        block, at = blocks[4 * k : 4 * k + 4], [shifted(x, cells) for x in v]
        terms.append([block[2 * f] * at[0] + block[2 * f + 1] * at[1] for f in (0, 1)])
    return plus(terms[1], plus(terms[0], terms[2]))


class Coarse:
    @staticmethod
    def build(coef, out, at=0, again=True):
        part = load(coef, 5, AGG)
        level = Level(part[0:2], part[2:4], part[4], chain_prev, chain_next)
        store(out, level.parts(), at * LEVEL_ROWS)
        if not again:
            return
        (l0, l1), (r0, r1), (i0, i1, i2) = level.left, level.faces, level.inv
        from_left = [i0 * l0, i2 * l1, i2 * l0, i1 * l1]
        from_right = [i0 * r0, i2 * r1, i2 * r0, i1 * r1]
        left_before, right_before = ([chain_prev(x) for x in b] for b in (from_left, from_right))
        left_after, right_after = ([chain_next(x) for x in b] for b in (from_left, from_right))
        keep = jnp.full_like(l0, KEEP * KEEP)
        zero = jnp.zeros_like(l0)
        twice = [
            *product(from_left, left_before),
            *plus(
                [keep, zero, zero, keep],
                plus(product(from_left, right_before), product(from_right, left_after)),
            ),
            *product(from_right, right_after),
        ]
        store(out, twice, at * LEVEL_ROWS + PARTS * AGG)

    def __init__(self, ref, at=0):
        self.ref, self.at = ref, at * LEVEL_ROWS
        self.level = Level.load(load(ref, PARTS, AGG, self.at), chain_prev, chain_next)

    def begin(self, source):
        field, inner = self.level.begin(source)
        return field, self.level.leftover(source, inner)

    def again(self, v, field):
        near = self.level.step(self.level.flow(v))
        far = apply_blocks(load(self.ref, TWICE, AGG, self.at + PARTS * AGG), v)
        return [(field[f] + far[f]) + (2.0 * KEEP) * near[f] for f in (0, 1)]


def store2(ref, v):
    ref[0:AGG, :] = v[0]
    ref[AGG : 2 * AGG, :] = v[1]


def load2(ref):
    return [ref[0:AGG, :], ref[AGG : 2 * AGG, :]]


def coef_kernel(token, face_hbm, sink_hbm, kap_hbm, out, level, face, sink, kap, sems):
    for copy in start_copies((face_hbm, sink_hbm, kap_hbm), (face, sink, kap), sems):
        copy.wait()
    faces, sinks = planar(face, AGG), planar(sink, AGG)
    last = last_cell((AGG, LANES))
    for f in (0, 1):
        out[f * AGG : (f + 1) * AGG, :] = jnp.where(last, 0.0, faces[f])
        out[(2 + f) * AGG : (3 + f) * AGG, :] = sinks[f]
    out[4 * AGG : 5 * AGG, :] = kap[...] * jnp.sqrt(sinks[0] * sinks[1])
    Coarse.build(out, level)


def pair_kernel(mine, other, out, level):
    out[...] = mine[...] + other[...]
    Coarse.build(out, level)


def upper_kernel(coef2, coef2_a, coef2_b, coef2_c, levels, near, far, top):
    near[...] = coef2[...] + coef2_a[...]
    far[...] = coef2_b[...] + coef2_c[...]
    top[...] = near[...] + far[...]
    for k, ref in enumerate((near, top, far)):
        Coarse.build(ref, levels, k, ref is not far)


def restrict_kernel(narrow, recv, level1, token, leftover, below, marks, own_edges):
    n = narrow[0]
    lane = iota((NARROW, LANES), 1)
    src = iota((NARROW, LANES), 0)
    raw = recv[pl.ds(2 * CAP, NARROW, stride=UNIT), :]
    code = jnp.where(lane >= LABEL, raw, 0.0).astype(I32)
    plain = jnp.where(code > 0, (code - 1) % AGG, -1)

    from_end = lane > 2 * SIDE * 7
    for q in range(7):
        from_end = from_end | ((lane >= 2 * SIDE * q) & (lane < 2 * SIDE * q + SIDE))
    cells = jnp.where(from_end, raw, pltpu.roll(raw, NARROW - 1, 0))
    data, source = interface_level(cells)
    _, inner = data.begin(source)
    mis = [pltpu.roll(m, LANES - SIDE, 1) for m in data.leftover(source, inner)]
    mis = jnp.concatenate(mis, axis=1)
    wide_lane = iota((NARROW, 2 * LANES), 1) % LANES
    real = iota((NARROW, 2 * LANES), 0) < NARROW - 1
    after_end = jnp.where((wide_lane >= LANES - 3) & real, mis, 0.0)
    at_start = jnp.where((wide_lane < 3) & real, mis, 0.0)
    is_end = code > 128
    is_start = (code > 64) & (code <= 128)
    end_at = jnp.max(jnp.where(is_end, plain, -1), axis=1, keepdims=True)
    start_at = jnp.max(jnp.where(is_start, plain, -1), axis=1, keepdims=True)
    end_hot = jnp.where(lane == end_at, 1.0, 0.0)
    start_hot = jnp.where(lane == start_at, 1.0, 0.0)
    start_next = pltpu.roll(start_hot, NARROW - 1, 0)
    zeros = jnp.zeros((2 * NARROW, LANES), F32)
    hot = jnp.transpose(jnp.concatenate([end_hot, start_next, zeros], axis=0), (1, 0))
    edge_hot = hot[0:AGG, :].astype(BF16)
    edge_rows = jnp.concatenate(
        [after_end, at_start, jnp.zeros((2 * NARROW, 2 * LANES), F32)], axis=0
    )

    rows = []
    for t in range(NARROW // 8):
        spread = pltpu.roll(plain[8 * t : 8 * t + 8], CAP, 1, stride=CAP, stride_axis=0)
        mine = jnp.where(lane[0:8] // CAP == src[0:8], spread, 0)
        rows.append(jnp.sum(mine, axis=0, keepdims=True))
    total = select_rows(edge_hot, edge_rows)
    for half in (0, 1):
        hots, parts = [], []
        for t in (2 * half, 2 * half + 1):
            hots.append(iota((AGG, LANES), 0) == rows[t])
            for s in range(8 * t, 8 * t + 8):
                parts.append(
                    jnp.concatenate(
                        [recv[pl.ds(s * UNIT + f, CAP, stride=2), :] for f in (0, 1)], axis=1
                    )
                )
        total = total + select_rows(
            as_bf16(jnp.concatenate(hots, axis=1)), jnp.concatenate(parts, axis=0)
        )
    source_c = [total[:, 0:LANES], total[:, LANES:]]
    correction, rest = Coarse(level1).begin(source_c)
    store2(leftover, rest)
    store2(below, correction)

    for t in range(NARROW // 8):
        marks[t : t + 1, :] = rows[t].astype(F32)
    marks[8 : 8 + NARROW, :] = pltpu.roll(end_hot, 1, 0)
    marks[8 + NARROW : 8 + 2 * NARROW, :] = start_next
    own_edges[0:1, :] = jnp.sum(jnp.where(src == n - 1, cells, 0.0), axis=0, keepdims=True)
    own_edges[1:2, :] = jnp.sum(jnp.where(src == n, cells, 0.0), axis=0, keepdims=True)


def second_kernel(mine, other, level2, leftover, below):
    source = [a + b for a, b in zip(load2(mine), load2(other))]
    correction, rest = Coarse(level2).begin(source)
    store2(leftover, rest)
    store2(below, correction)


def side_kernel(marks, own_edges, hot, edges):
    lane = iota((LANES, LANES), 1)
    for t in range(NARROW // 8):
        mark = jnp.broadcast_to(marks[t : t + 1, :], (LANES, LANES))
        mark = jnp.transpose(mark, (1, 0)).astype(I32)
        once = as_bf16(mark == lane % AGG)
        last = as_bf16((mark == lane) & (lane < AGG))
        hot[t * LANES : (t + 1) * LANES, 0:LANES] = once
        hot[t * LANES : (t + 1) * LANES, LANES:] = last
    ends = marks[8 : 8 + 2 * NARROW, :]
    hot[NARROW * CAP :, 0:LANES] = (ends + pltpu.roll(ends, AGG, 1)).astype(BF16)
    hot[NARROW * CAP :, LANES:] = ends.astype(BF16)
    data, source = interface_level(own_edges[...])
    field, _ = data.begin(source)
    store(edges, [*field, *data.parts()])


def top_kernel(
    left2, left2_a, left2_b, left2_c, levels, level2, below2, level1, below1, hot, out
):
    source3 = [a + b for a, b in zip(load2(left2), load2(left2_a))]
    source3_far = [a + b for a, b in zip(load2(left2_b), load2(left2_c))]
    level3, level4, level3_far = [Coarse(levels, k) for k in range(3)]
    below3, rest = level3.begin(source3)
    _, rest_far = level3_far.begin(source3_far)
    v, _ = level4.begin(plus(rest, rest_far))
    v = level4.again(v, v)
    for level, field in (
        (level3, below3),
        (Coarse(level2), load2(below2)),
        (Coarse(level1), load2(below1)),
    ):
        v = level.again(plus(field, v), field)

    both = jnp.concatenate([v[0], v[1]], axis=1)
    both = jnp.concatenate([*split3(both), jnp.zeros((AGG, 2 * LANES), BF16)], axis=0)
    rows = jnp.dot(hot[...], both, preferred_element_type=F32)
    for s in range(NARROW):
        for f in (0, 1):
            out[pl.ds(s * UNIT + f, CAP, stride=2), :] = rows[
                s * CAP : (s + 1) * CAP, f * LANES : (f + 1) * LANES
            ]
    ends = rows[NARROW * CAP :, :]
    lane = iota((NARROW, LANES), 1)
    halo = []
    for f in (0, 1):
        part = ends[:, f * LANES : (f + 1) * LANES]
        halo.append(jnp.where(lane >= LANES // 2, part[0:NARROW], part[NARROW:]))
    middle = (lane >= LANES // 4) & (lane < LANES * 3 // 4)
    out[pl.ds(2 * CAP, NARROW, stride=UNIT), :] = jnp.where(
        middle, pltpu.roll(halo[1], LANES // 2, 1), halo[0]
    )


def post_kernel(narrow, fine, slots, recv, edges, out):
    n = narrow[0]
    field = load(fine, 2, BLK)
    data = Level.load(load(fine, PARTS, BLK, 2 * BLK), chain_prev, chain_next)
    slot = slots[...].astype(I32)
    lane = iota((BLK, LANES), 1)
    lifted = None
    for half in (0, 1):
        hots, parts = [], []
        for t in (2 * half, 2 * half + 1):
            hots.append(slot == lane + t * LANES)
            for s in range(8 * t, 8 * t + 8):
                parts.append(
                    jnp.concatenate(
                        [recv[pl.ds(s * UNIT + f, CAP, stride=2), :] for f in (0, 1)], axis=1
                    )
                )
        term = select_rows(as_bf16(jnp.concatenate(hots, axis=1)), jnp.concatenate(parts, axis=0))
        lifted = term if lifted is None else lifted + term
    lifted = [lifted[:, 0:LANES], lifted[:, LANES:]]
    v = data.again([a + b for a, b in zip(field, lifted)], field)

    edge_field = load(edges, 2, 8)
    edge_data = Level.load(load(edges, PARTS, 8, 16), row_prev, row_next)
    lane1 = iota((1, LANES), 1)
    row8 = iota((8, LANES), 0)
    edge_v = []
    halo = jnp.sum(recv[pl.ds(2 * CAP, NARROW, stride=UNIT), :], axis=0, keepdims=True)
    for f in (0, 1):
        beyond = halo if f == 0 else pltpu.roll(halo, LANES // 2, 1)
        first = jnp.where(lane1 >= LANES // 2, beyond, lifted[f][0:1, :])
        final = jnp.where(lane1 >= LANES // 2, lifted[f][BLK - 1 : BLK, :], beyond)
        lift = jnp.where(row8 == 0, first, jnp.where(row8 == 1, final, 0.0))
        lift = jnp.where(iota((8, LANES), 1) < 2 * SIDE, pltpu.roll(lift, SIDE, 1), 0.0)
        edge_v.append(edge_field[f] + lift)
    edge_v = edge_data.again(edge_v, edge_field)
    for f in (0, 1):
        out[pl.ds(f, BLK, stride=2), :] = v[f]
        moved = pltpu.roll(edge_v[f], LANES - SIDE, 1)
        out[f : f + 1, :] = jnp.where((lane1 < 4) & (n > 0), moved[0:1, :], v[f][0:1, :])
        final = 2 * (BLK - 1) + f
        out[final : final + 1, :] = jnp.where(
            (lane1 >= LANES - 4) & (n < NARROW - 1), moved[1:2, :], v[f][BLK - 1 : BLK, :]
        )


def call(kernel, outs, *args, spaces=(), scratch=(), cost=None):
    spaces = (*spaces, *[pltpu.VMEM] * (len(args) - len(spaces)))
    args = [
        pltpu.with_memory_space_constraint(a, s) if s == pltpu.HBM else a
        for a, s in zip(args, spaces)
    ]
    return pl.pallas_call(
        kernel,
        out_shape=[jax.ShapeDtypeStruct(s, k) for s, k in outs],
        in_specs=[pl.BlockSpec(memory_space=space) for space in spaces],
        out_specs=[pl.BlockSpec(memory_space=pltpu.VMEM) for _ in outs],
        scratch_shapes=scratch,
        cost_estimate=cost,
        compiler_params=pltpu.CompilerParams(vmem_limit_bytes=32 * 1024 * 1024),
    )(*args)


def exchange(value, bits):
    return lax.ppermute(value, "wide", [(i, i ^ bits) for i in range(lax.axis_size("wide"))])


def to_all(units):
    shape = (NARROW * UNIT, 1, LANES)
    moved = lax.all_to_all(units.reshape(shape), "narrow", 0, 0, tiled=True)
    return moved.reshape(NARROW * UNIT, LANES)


def on_device(
    rhs, fine_face, fine_sink, fine_kap, cell_mask, block_aggregate, coarse_face, coarse_sink, coarse_kap
):
    narrow = lax.axis_index("narrow").astype(I32).reshape(1)
    cells = ((2 * BLK, LANES), F32)
    five, level, two = (5 * AGG, LANES), (LEVEL_ROWS, LANES), (2 * AGG, LANES)
    five, level, two = (five, F32), (level, F32), (two, F32)
    units = ((NARROW * UNIT, LANES), F32)
    vmem = lambda *rows: [pltpu.VMEM((r, LANES), F32) for r in rows]
    held = vmem(2 * BLK, 2 * BLK, 2 * BLK, BLK) + [pltpu.VMEM((BLK, LANES), I32)]
    beside = pl.CostEstimate(flops=0, bytes_accessed=4 * 1024 * 1024, transcendentals=0)
    fine_args = (
        rhs.reshape(2 * BLK, LANES),
        fine_face.reshape(2 * BLK, LANES),
        fine_sink.reshape(2 * BLK, LANES),
        fine_kap,
        cell_mask,
    )
    sent, slot_row = call(
        pre_kernel,
        [units, ((8, BLK), F32)],
        narrow,
        block_aggregate.reshape(1, BLK),
        *fine_args,
        spaces=(pltpu.SMEM, *[pltpu.HBM] * 6),
        scratch=held + [pltpu.VMEM((1, BLK), I32), pltpu.SemaphoreType.DMA((6,))],
    )
    recv = to_all(sent)
    coef1, level1 = call(
        coef_kernel,
        [five, level],
        slot_row,
        coarse_face.reshape(2 * AGG, LANES),
        coarse_sink.reshape(2 * AGG, LANES),
        coarse_kap,
        spaces=(pltpu.VMEM, *[pltpu.HBM] * 3),
        scratch=vmem(2 * AGG, 2 * AGG, AGG) + [pltpu.SemaphoreType.DMA((3,))],
        cost=beside,
    )
    fine, slots = call(
        ready_kernel,
        [((9 * BLK, LANES), F32), ((BLK, LANES), F32)],
        slot_row,
        *fine_args,
        spaces=(pltpu.VMEM, *[pltpu.HBM] * 5),
        scratch=held + [pltpu.SemaphoreType.DMA((5,))],
        cost=beside,
    )
    coef2, level2 = call(pair_kernel, [five, level], coef1, exchange(coef1, 1), cost=beside)
    (levels,) = call(
        upper_kernel,
        [((2 * LEVEL_ROWS + PARTS * AGG, LANES), F32)],
        coef2,
        *[exchange(coef2, b) for b in (2, 6, 4)],
        scratch=vmem(5 * AGG, 5 * AGG, 5 * AGG),
        cost=beside,
    )
    left1, below1, marks, own_edges = call(
        restrict_kernel,
        [two, two, ((8 + 2 * NARROW, LANES), F32), ((8, LANES), F32)],
        narrow,
        recv,
        level1,
        fine,
        spaces=(pltpu.SMEM,),
    )
    hot, edges = call(
        side_kernel,
        [((NARROW * CAP + 2 * NARROW, 2 * LANES), BF16), ((9 * 8, LANES), F32)],
        marks,
        own_edges,
    )
    left2, below2 = call(
        second_kernel, [two, two], left1, exchange(left1, 1), level2
    )
    (back,) = call(
        top_kernel,
        [units],
        left2,
        *[exchange(left2, b) for b in (2, 6, 4)],
        levels,
        level2,
        below2,
        level1,
        below1,
        hot,
    )
    recv = to_all(back)
    (out,) = call(post_kernel, [cells], narrow, fine, slots, recv, edges, spaces=(pltpu.SMEM,))
    return out.reshape(BLK, 2, LANES)


def solution(mesh):
    both = ("wide", "narrow")
    placed = (
        P(both, None, None),
        P(both, None, None),
        P(both, None, None),
        P(both, None),
        P(both, None),
        P(both),
        P(both, None, None),
        P(both, None, None),
        P(both, None),
    )
    return jax.shard_map(
        on_device,
        mesh=mesh,
        in_specs=placed,
        out_specs=P(both, None, None),
        check_vma=False,
    )
```

```python
import jax
import jax.numpy as jnp
from jax import lax
from jax.experimental import pallas as pl
from jax.experimental.pallas import tpu as pltpu
from jax.sharding import PartitionSpec as P

OMEGA = 0.8
KEEP = 1.0 - OMEGA
LANES = 128
BLK = 256
AGG = 64
NARROW = 32
CAP = 16
UNIT = 2 * CAP + 1
SIDE = 7
LABEL = LANES - CAP
F32, BF16, I32 = jnp.float32, jnp.bfloat16, jnp.int32


def iota(shape, dim):
    return lax.broadcasted_iota(I32, shape, dim)


def chain_next(v):
    ahead = pltpu.roll(v, LANES - 1, 1)
    below = pltpu.roll(ahead, v.shape[0] - 1, 0)
    return jnp.where(iota(v.shape, 1) == LANES - 1, below, ahead)


def chain_prev(v):
    behind = pltpu.roll(v, 1, 1)
    above = pltpu.roll(behind, 1, 0)
    return jnp.where(iota(v.shape, 1) == 0, above, behind)


def row_next(v):
    return pltpu.roll(v, LANES - 1, 1)


def row_prev(v):
    return pltpu.roll(v, 1, 1)


class Level:
    def __init__(self, faces, sinks, coupling, prev, nxt, left=None):
        self.prev, self.nxt = prev, nxt
        self.faces = faces
        self.left = [prev(f) for f in faces] if left is None else left
        diag = [s + l + f for s, l, f in zip(sinks, self.left, faces)]
        scale = OMEGA / (diag[0] * diag[1] - coupling * coupling)
        self.inv = [diag[1] * scale, diag[0] * scale, coupling * scale]

    def parts(self):
        return [*self.faces, *self.left, *self.inv]

    @classmethod
    def load(cls, part, prev, nxt):
        level = cls.__new__(cls)
        level.prev, level.nxt = prev, nxt
        level.faces, level.left, level.inv = part[0:2], part[2:4], part[4:7]
        return level

    def flow(self, v):
        return [self.left[f] * self.prev(v[f]) + self.faces[f] * self.nxt(v[f]) for f in (0, 1)]

    def step(self, r):
        return [
            self.inv[0] * r[0] + self.inv[2] * r[1],
            self.inv[2] * r[0] + self.inv[1] * r[1],
        ]

    def begin(self, source):
        g = self.step(source)
        w = self.step(self.flow(g))
        field = [(1.0 + KEEP) * a + b for a, b in zip(g, w)]
        return field, [(2.0 * KEEP) * a + b for a, b in zip(g, w)]

    def leftover(self, source, inner):
        return [(KEEP * KEEP) * a + b for a, b in zip(source, self.flow(inner))]

    def again(self, v, field):
        u = self.step(self.flow(v))
        d = self.step(self.flow([(2.0 * KEEP) * a + b for a, b in zip(v, u)]))
        return [(field[f] + (KEEP * KEEP) * v[f]) + d[f] for f in (0, 1)]


def store(ref, parts, at=0):
    for part in parts:
        ref[at : at + part.shape[0], :] = part
        at += part.shape[0]


def load(ref, count, rows, at=0):
    return [ref[at + k * rows : at + (k + 1) * rows, :] for k in range(count)]


def last_cell(shape):
    return (iota(shape, 0) == shape[0] - 1) & (iota(shape, 1) == LANES - 1)


def split3(x):
    hi = x.astype(BF16)
    rest = x - hi.astype(F32)
    mid = rest.astype(BF16)
    return hi, mid, (rest - mid.astype(F32)).astype(BF16)


def select_rows(onehot, x):
    return jnp.dot(
        jnp.concatenate([onehot] * 3, axis=1),
        jnp.concatenate(split3(x), axis=0),
        preferred_element_type=F32,
    )


def as_bf16(mask):
    return jnp.where(mask, 1.0, 0.0).astype(BF16)


def planar(ref, rows):
    return [ref[pl.ds(f, rows, stride=2), :] for f in (0, 1)]


def start_copies(sources, targets, sems):
    copies = [
        pltpu.make_async_copy(a, b, sems.at[k]) for k, (a, b) in enumerate(zip(sources, targets))
    ]
    for copy in copies:
        copy.start()
    return copies


def fine_start(rhs, face, sink, kap, mask):
    live = mask[...].astype(F32)
    live_next = jnp.where(last_cell((BLK, LANES)), 0.0, chain_next(live))
    both = live * live_next
    sinks = planar(sink, BLK)
    coupling = kap[...] * jnp.sqrt(sinks[0] * sinks[1]) * live
    data = Level([f * both for f in planar(face, BLK)], sinks, coupling, chain_prev, chain_next)
    source = [r * live for r in planar(rhs, BLK)]
    return data, coupling, source, *data.begin(source)


def ready_kernel(slot_row, *refs):
    inputs, fine, slots, held = refs[0:5], refs[5], refs[6], refs[7:12]
    sems, stage = refs[12:14]
    copies = start_copies(inputs, held, sems)
    slots[...] = jnp.transpose(jnp.broadcast_to(slot_row[0:1, :], (LANES, BLK)), (1, 0))
    for copy in copies:
        copy.wait()
    data, _, _, field, _ = fine_start(*held)
    store(stage, [*field, *data.parts()])
    push = pltpu.make_async_copy(stage, fine, sems.at[0])
    push.start()
    push.wait()


def pre_kernel(narrow, agg_hbm, *refs):
    inputs, out, slots, held, sems = refs[0:5], refs[5], refs[6], refs[7:13], refs[13]
    rhs, face, sink, kap, mask, agg = held
    n = narrow[0]
    for copy in start_copies((*inputs, agg_hbm), held, sems):
        copy.wait()

    label = agg[...]
    owner = label // AGG
    within = label - owner * AGG
    owned = iota((NARROW, BLK), 0) == owner
    before = as_bf16(iota((BLK, BLK), 0) < iota((BLK, BLK), 1))
    counts = jnp.dot(as_bf16(owned), before, preferred_element_type=F32)
    rank = jnp.sum(jnp.where(owned, counts, 0.0), axis=0, keepdims=True).astype(I32)
    slot = owner * CAP + rank
    put = as_bf16(iota((NARROW * CAP, BLK), 0) == slot)

    block = iota((1, BLK), 1)
    code = within + 1 + jnp.where(block == 0, 64, 0) + jnp.where(block == BLK - 1, 128, 0)
    coded = jnp.where(owned, code.astype(F32), 0.0).astype(BF16)
    at_rank = as_bf16(iota((LANES, BLK), 0) % CAP == rank)
    labels = lax.dot_general(
        coded, at_rank, (((1,), (1,)), ((), ())), preferred_element_type=F32
    )
    slots[...] = jnp.broadcast_to(slot.astype(F32), (8, BLK))

    data, coupling, source, _, inner = fine_start(rhs, face, sink, kap, mask)
    misfit = data.leftover(source, inner)
    row, lane = iota((BLK, LANES), 0), iota((BLK, LANES), 1)
    drop = ((row == BLK - 1) & (lane >= LANES - 3) & (n < NARROW - 1)) | (
        (row == 0) & (lane < 3) & (n > 0)
    )
    misfit = jnp.concatenate([jnp.where(drop, 0.0, m) for m in misfit], axis=1)

    rows = select_rows(put, misfit)
    for o in range(NARROW):
        for f in (0, 1):
            out[pl.ds(o * UNIT + f, CAP, stride=2), :] = rows[
                o * CAP : (o + 1) * CAP, f * LANES : (f + 1) * LANES
            ]

    lane1 = iota((1, LANES), 1)

    def ends(final, first):
        return jnp.where(lane1 >= LANES // 2, final, first)

    def rows_of(v):
        return ends(v[BLK - 1 : BLK, :], v[0:1, :])

    live_first = mask[0:1, :].astype(F32)
    live_final = mask[BLK - 1 : BLK, :].astype(F32)
    faces = []
    for f in (0, 1):
        open_face = face[2 * (BLK - 1) + f : 2 * (BLK - 1) + f + 1, :] * live_final
        final = jnp.where(lane1 == LANES - 1, open_face, data.faces[f][BLK - 1 : BLK, :])
        faces.append(ends(final, data.faces[f][0:1, :]))
    sinks = [
        ends(sink[2 * (BLK - 1) + f : 2 * (BLK - 1) + f + 1, :], sink[f : f + 1, :]) for f in (0, 1)
    ]
    quantities = [*map(rows_of, source), *faces, *sinks, rows_of(coupling)]
    edges = jnp.zeros((1, LANES), F32)
    for q, cells in enumerate(quantities):
        here = (lane1 >= 2 * SIDE * q) & (lane1 < 2 * SIDE * (q + 1))
        edges = jnp.where(here, pltpu.roll(cells, 2 * SIDE * q + SIDE, 1), edges)
    spare = 2 * SIDE * len(quantities)
    edges = jnp.where(lane1 == spare, pltpu.roll(live_first, spare, 1), edges)
    for f in (0, 1):
        before = pltpu.roll(faces[f], spare + 1 + f + SIDE + 1, 1)
        edges = jnp.where(lane1 == spare + 1 + f, before, edges)
    out[pl.ds(2 * CAP, NARROW, stride=UNIT), :] = jnp.where(
        iota((NARROW, LANES), 1) >= LABEL, labels, edges
    )


def interface_level(cells):
    lane = iota(cells.shape, 1)
    spare = 2 * SIDE * 7

    def moved(start, to):
        shift = (to - start) % LANES
        return cells if shift == 0 else pltpu.roll(cells, shift, 1)

    def quantity(q, fill):
        return jnp.where(lane < 2 * SIDE, moved(2 * SIDE * q, 0), fill)

    source = [quantity(0, 0.0), quantity(1, 0.0)]
    live_next = jnp.where(lane == SIDE - 1, moved(spare, SIDE - 1), 1.0)
    faces = [quantity(2, 0.0) * live_next, quantity(3, 0.0) * live_next]
    left = [
        jnp.where(lane == 0, moved(spare + 1 + f, 0), row_prev(faces[f])) for f in (0, 1)
    ]
    sinks = [quantity(4, 1.0), quantity(5, 1.0)]
    return Level(faces, sinks, quantity(6, 0.0), row_prev, row_next, left), source


PARTS = 7
REACH = (2, 0, -2)
TWICE = 4 * len(REACH)
LEVEL_ROWS = (PARTS + 2 * TWICE) * AGG


def shifted(v, cells):
    if cells == 0:
        return v
    moved = pltpu.roll(v, cells % LANES, 1)
    lane = iota(v.shape, 1)
    if cells > 0:
        return jnp.where(lane < cells, pltpu.roll(moved, 1, 0), moved)
    return jnp.where(lane >= LANES + cells, pltpu.roll(moved, v.shape[0] - 1, 0), moved)


def product(a, b):
    return [
        a[0] * b[0] + a[1] * b[2],
        a[0] * b[1] + a[1] * b[3],
        a[2] * b[0] + a[3] * b[2],
        a[2] * b[1] + a[3] * b[3],
    ]


def scaled(rows, b):
    return [rows[0] * b[0], rows[0] * b[1], rows[1] * b[2], rows[1] * b[3]]


def plus(a, b):
    return [x + y for x, y in zip(a, b)]


def apply_blocks(blocks, v):
    terms = []
    for k, cells in enumerate(REACH):
        block, at = blocks[4 * k : 4 * k + 4], [shifted(x, cells) for x in v]
        terms.append([block[2 * f] * at[0] + block[2 * f + 1] * at[1] for f in (0, 1)])
    return plus(terms[1], plus(terms[0], terms[2]))


class Coarse:
    @staticmethod
    def build(coef, out, at=0, again=True):
        part = load(coef, 5, AGG)
        level = Level(part[0:2], part[2:4], part[4], chain_prev, chain_next)
        store(out, level.parts(), at * LEVEL_ROWS)
        if not again:
            return
        (l0, l1), (r0, r1), (i0, i1, i2) = level.left, level.faces, level.inv
        from_left = [i0 * l0, i2 * l1, i2 * l0, i1 * l1]
        from_right = [i0 * r0, i2 * r1, i2 * r0, i1 * r1]
        left_before, right_before = ([chain_prev(x) for x in b] for b in (from_left, from_right))
        left_after, right_after = ([chain_next(x) for x in b] for b in (from_left, from_right))
        keep = jnp.full_like(l0, KEEP * KEEP)
        zero = jnp.zeros_like(l0)
        twice = [
            *product(from_left, left_before),
            *plus(
                [keep, zero, zero, keep],
                plus(product(from_left, right_before), product(from_right, left_after)),
            ),
            *product(from_right, right_after),
        ]
        left, right = (l0, l1), (r0, r1)
        rest = [
            *scaled(left, left_before),
            *plus(scaled(left, right_before), scaled(right, left_after)),
            *scaled(right, right_after),
        ]
        store(out, [*twice, *rest], at * LEVEL_ROWS + PARTS * AGG)

    def __init__(self, ref, at=0):
        self.ref, self.at = ref, at * LEVEL_ROWS
        self.level = Level.load(load(ref, PARTS, AGG, self.at), chain_prev, chain_next)

    def begin(self, source):
        g = self.level.step(source)
        near = self.level.flow(g)
        field = [(1.0 + KEEP) * a + b for a, b in zip(g, self.level.step(near))]
        far = apply_blocks(load(self.ref, TWICE, AGG, self.at + (PARTS + TWICE) * AGG), g)
        rest = [
            ((KEEP * KEEP) * a + b) + (2.0 * KEEP) * c for a, b, c in zip(source, far, near)
        ]
        return field, rest

    def again(self, v, field):
        near = self.level.step(self.level.flow(v))
        far = apply_blocks(load(self.ref, TWICE, AGG, self.at + PARTS * AGG), v)
        return [(field[f] + far[f]) + (2.0 * KEEP) * near[f] for f in (0, 1)]


def store2(ref, v):
    ref[0:AGG, :] = v[0]
    ref[AGG : 2 * AGG, :] = v[1]


def load2(ref):
    return [ref[0:AGG, :], ref[AGG : 2 * AGG, :]]


def coef_kernel(token, face_hbm, sink_hbm, kap_hbm, out, level, face, sink, kap, sems):
    for copy in start_copies((face_hbm, sink_hbm, kap_hbm), (face, sink, kap), sems):
        copy.wait()
    faces, sinks = planar(face, AGG), planar(sink, AGG)
    last = last_cell((AGG, LANES))
    for f in (0, 1):
        out[f * AGG : (f + 1) * AGG, :] = jnp.where(last, 0.0, faces[f])
        out[(2 + f) * AGG : (3 + f) * AGG, :] = sinks[f]
    out[4 * AGG : 5 * AGG, :] = kap[...] * jnp.sqrt(sinks[0] * sinks[1])
    Coarse.build(out, level)


def pair_kernel(mine, other, out, level):
    out[...] = mine[...] + other[...]
    Coarse.build(out, level)


def upper_kernel(coef2, coef2_a, coef2_b, coef2_c, levels, near, far, top):
    near[...] = coef2[...] + coef2_a[...]
    far[...] = coef2_b[...] + coef2_c[...]
    top[...] = near[...] + far[...]
    for k, ref in enumerate((near, top, far)):
        Coarse.build(ref, levels, k, ref is not far)


def restrict_kernel(narrow, recv, level1, token, leftover, below, marks, own_edges):
    n = narrow[0]
    lane = iota((NARROW, LANES), 1)
    src = iota((NARROW, LANES), 0)
    raw = recv[pl.ds(2 * CAP, NARROW, stride=UNIT), :]
    code = jnp.where(lane >= LABEL, raw, 0.0).astype(I32)
    plain = jnp.where(code > 0, (code - 1) % AGG, -1)

    from_end = lane > 2 * SIDE * 7
    for q in range(7):
        from_end = from_end | ((lane >= 2 * SIDE * q) & (lane < 2 * SIDE * q + SIDE))
    cells = jnp.where(from_end, raw, pltpu.roll(raw, NARROW - 1, 0))
    data, source = interface_level(cells)
    _, inner = data.begin(source)
    mis = [pltpu.roll(m, LANES - SIDE, 1) for m in data.leftover(source, inner)]
    mis = jnp.concatenate(mis, axis=1)
    wide_lane = iota((NARROW, 2 * LANES), 1) % LANES
    real = iota((NARROW, 2 * LANES), 0) < NARROW - 1
    after_end = jnp.where((wide_lane >= LANES - 3) & real, mis, 0.0)
    at_start = jnp.where((wide_lane < 3) & real, mis, 0.0)
    is_end = code > 128
    is_start = (code > 64) & (code <= 128)
    end_at = jnp.max(jnp.where(is_end, plain, -1), axis=1, keepdims=True)
    start_at = jnp.max(jnp.where(is_start, plain, -1), axis=1, keepdims=True)
    end_hot = jnp.where(lane == end_at, 1.0, 0.0)
    start_hot = jnp.where(lane == start_at, 1.0, 0.0)
    start_next = pltpu.roll(start_hot, NARROW - 1, 0)
    zeros = jnp.zeros((2 * NARROW, LANES), F32)
    hot = jnp.transpose(jnp.concatenate([end_hot, start_next, zeros], axis=0), (1, 0))
    edge_hot = hot[0:AGG, :].astype(BF16)
    edge_rows = jnp.concatenate(
        [after_end, at_start, jnp.zeros((2 * NARROW, 2 * LANES), F32)], axis=0
    )

    rows = []
    for t in range(NARROW // 8):
        spread = pltpu.roll(plain[8 * t : 8 * t + 8], CAP, 1, stride=CAP, stride_axis=0)
        mine = jnp.where(lane[0:8] // CAP == src[0:8], spread, 0)
        rows.append(jnp.sum(mine, axis=0, keepdims=True))
    total = select_rows(edge_hot, edge_rows)
    for half in (0, 1):
        hots, parts = [], []
        for t in (2 * half, 2 * half + 1):
            hots.append(iota((AGG, LANES), 0) == rows[t])
            for s in range(8 * t, 8 * t + 8):
                parts.append(
                    jnp.concatenate(
                        [recv[pl.ds(s * UNIT + f, CAP, stride=2), :] for f in (0, 1)], axis=1
                    )
                )
        total = total + select_rows(
            as_bf16(jnp.concatenate(hots, axis=1)), jnp.concatenate(parts, axis=0)
        )
    source_c = [total[:, 0:LANES], total[:, LANES:]]
    correction, rest = Coarse(level1).begin(source_c)
    store2(leftover, rest)
    store2(below, correction)

    for t in range(NARROW // 8):
        marks[t : t + 1, :] = rows[t].astype(F32)
    marks[8 : 8 + NARROW, :] = pltpu.roll(end_hot, 1, 0)
    marks[8 + NARROW : 8 + 2 * NARROW, :] = start_next
    own_edges[0:1, :] = jnp.sum(jnp.where(src == n - 1, cells, 0.0), axis=0, keepdims=True)
    own_edges[1:2, :] = jnp.sum(jnp.where(src == n, cells, 0.0), axis=0, keepdims=True)


def second_kernel(mine, other, level2, leftover, below):
    source = [a + b for a, b in zip(load2(mine), load2(other))]
    correction, rest = Coarse(level2).begin(source)
    store2(leftover, rest)
    store2(below, correction)


def side_kernel(marks, own_edges, hot, edges):
    lane = iota((LANES, LANES), 1)
    for t in range(NARROW // 8):
        mark = jnp.broadcast_to(marks[t : t + 1, :], (LANES, LANES))
        mark = jnp.transpose(mark, (1, 0)).astype(I32)
        once = as_bf16(mark == lane % AGG)
        last = as_bf16((mark == lane) & (lane < AGG))
        hot[t * LANES : (t + 1) * LANES, 0:LANES] = once
        hot[t * LANES : (t + 1) * LANES, LANES:] = last
    ends = marks[8 : 8 + 2 * NARROW, :]
    hot[NARROW * CAP :, 0:LANES] = (ends + pltpu.roll(ends, AGG, 1)).astype(BF16)
    hot[NARROW * CAP :, LANES:] = ends.astype(BF16)
    data, source = interface_level(own_edges[...])
    field, _ = data.begin(source)
    store(edges, [*field, *data.parts()])


def top_kernel(
    left2, left2_a, left2_b, left2_c, levels, level2, below2, level1, below1, hot, out
):
    source3 = [a + b for a, b in zip(load2(left2), load2(left2_a))]
    source3_far = [a + b for a, b in zip(load2(left2_b), load2(left2_c))]
    level3, level4, level3_far = [Coarse(levels, k) for k in range(3)]
    below3, rest = level3.begin(source3)
    rest_far = level3_far.level.leftover(source3_far, level3_far.level.begin(source3_far)[1])
    v, _ = level4.begin(plus(rest, rest_far))
    v = level4.again(v, v)
    for level, field in (
        (level3, below3),
        (Coarse(level2), load2(below2)),
        (Coarse(level1), load2(below1)),
    ):
        v = level.again(plus(field, v), field)

    both = jnp.concatenate([v[0], v[1]], axis=1)
    both = jnp.concatenate([*split3(both), jnp.zeros((AGG, 2 * LANES), BF16)], axis=0)
    rows = jnp.dot(hot[...], both, preferred_element_type=F32)
    for s in range(NARROW):
        for f in (0, 1):
            out[pl.ds(s * UNIT + f, CAP, stride=2), :] = rows[
                s * CAP : (s + 1) * CAP, f * LANES : (f + 1) * LANES
            ]
    ends = rows[NARROW * CAP :, :]
    lane = iota((NARROW, LANES), 1)
    halo = []
    for f in (0, 1):
        part = ends[:, f * LANES : (f + 1) * LANES]
        halo.append(jnp.where(lane >= LANES // 2, part[0:NARROW], part[NARROW:]))
    middle = (lane >= LANES // 4) & (lane < LANES * 3 // 4)
    out[pl.ds(2 * CAP, NARROW, stride=UNIT), :] = jnp.where(
        middle, pltpu.roll(halo[1], LANES // 2, 1), halo[0]
    )


def post_kernel(narrow, fine, slots, recv, edges, out):
    n = narrow[0]
    field = load(fine, 2, BLK)
    data = Level.load(load(fine, PARTS, BLK, 2 * BLK), chain_prev, chain_next)
    slot = slots[...].astype(I32)
    lane = iota((BLK, LANES), 1)
    lifted = None
    for half in (0, 1):
        hots, parts = [], []
        for t in (2 * half, 2 * half + 1):
            hots.append(slot == lane + t * LANES)
            for s in range(8 * t, 8 * t + 8):
                parts.append(
                    jnp.concatenate(
                        [recv[pl.ds(s * UNIT + f, CAP, stride=2), :] for f in (0, 1)], axis=1
                    )
                )
        term = select_rows(as_bf16(jnp.concatenate(hots, axis=1)), jnp.concatenate(parts, axis=0))
        lifted = term if lifted is None else lifted + term
    lifted = [lifted[:, 0:LANES], lifted[:, LANES:]]
    v = data.again([a + b for a, b in zip(field, lifted)], field)

    edge_field = load(edges, 2, 8)
    edge_data = Level.load(load(edges, PARTS, 8, 16), row_prev, row_next)
    lane1 = iota((1, LANES), 1)
    row8 = iota((8, LANES), 0)
    edge_v = []
    halo = jnp.sum(recv[pl.ds(2 * CAP, NARROW, stride=UNIT), :], axis=0, keepdims=True)
    for f in (0, 1):
        beyond = halo if f == 0 else pltpu.roll(halo, LANES // 2, 1)
        first = jnp.where(lane1 >= LANES // 2, beyond, lifted[f][0:1, :])
        final = jnp.where(lane1 >= LANES // 2, lifted[f][BLK - 1 : BLK, :], beyond)
        lift = jnp.where(row8 == 0, first, jnp.where(row8 == 1, final, 0.0))
        lift = jnp.where(iota((8, LANES), 1) < 2 * SIDE, pltpu.roll(lift, SIDE, 1), 0.0)
        edge_v.append(edge_field[f] + lift)
    edge_v = edge_data.again(edge_v, edge_field)
    for f in (0, 1):
        out[pl.ds(f, BLK, stride=2), :] = v[f]
        moved = pltpu.roll(edge_v[f], LANES - SIDE, 1)
        out[f : f + 1, :] = jnp.where((lane1 < 4) & (n > 0), moved[0:1, :], v[f][0:1, :])
        final = 2 * (BLK - 1) + f
        out[final : final + 1, :] = jnp.where(
            (lane1 >= LANES - 4) & (n < NARROW - 1), moved[1:2, :], v[f][BLK - 1 : BLK, :]
        )


def call(kernel, outs, *args, spaces=(), scratch=(), cost=None, out_spaces=None):
    spaces = (*spaces, *[pltpu.VMEM] * (len(args) - len(spaces)))
    args = [
        pltpu.with_memory_space_constraint(a, s) if s == pltpu.HBM else a
        for a, s in zip(args, spaces)
    ]
    return pl.pallas_call(
        kernel,
        out_shape=[
            pltpu.HBM(s, k) if space == pltpu.HBM else jax.ShapeDtypeStruct(s, k)
            for (s, k), space in zip(outs, out_spaces or [pltpu.VMEM] * len(outs))
        ],
        in_specs=[pl.BlockSpec(memory_space=space) for space in spaces],
        out_specs=[
            pl.BlockSpec(memory_space=space) for space in out_spaces or [pltpu.VMEM] * len(outs)
        ],
        scratch_shapes=scratch,
        cost_estimate=cost,
        compiler_params=pltpu.CompilerParams(vmem_limit_bytes=32 * 1024 * 1024),
    )(*args)


def exchange(value, bits):
    return lax.ppermute(value, "wide", [(i, i ^ bits) for i in range(lax.axis_size("wide"))])


def to_all(units):
    shape = (NARROW * UNIT, 1, LANES)
    moved = lax.all_to_all(units.reshape(shape), "narrow", 0, 0, tiled=True)
    return moved.reshape(NARROW * UNIT, LANES)


def on_device(
    rhs, fine_face, fine_sink, fine_kap, cell_mask, block_aggregate, coarse_face, coarse_sink, coarse_kap
):
    narrow = lax.axis_index("narrow").astype(I32).reshape(1)
    cells = ((2 * BLK, LANES), F32)
    five, level, two = (5 * AGG, LANES), (LEVEL_ROWS, LANES), (2 * AGG, LANES)
    five, level, two = (five, F32), (level, F32), (two, F32)
    units = ((NARROW * UNIT, LANES), F32)
    vmem = lambda *rows: [pltpu.VMEM((r, LANES), F32) for r in rows]
    held = vmem(2 * BLK, 2 * BLK, 2 * BLK, BLK) + [pltpu.VMEM((BLK, LANES), I32)]
    beside = pl.CostEstimate(flops=0, bytes_accessed=4 * 1024 * 1024, transcendentals=0)
    fine_args = (
        rhs.reshape(2 * BLK, LANES),
        fine_face.reshape(2 * BLK, LANES),
        fine_sink.reshape(2 * BLK, LANES),
        fine_kap,
        cell_mask,
    )
    sent, slot_row = call(
        pre_kernel,
        [units, ((8, BLK), F32)],
        narrow,
        block_aggregate.reshape(1, BLK),
        *fine_args,
        spaces=(pltpu.SMEM, *[pltpu.HBM] * 6),
        scratch=held + [pltpu.VMEM((1, BLK), I32), pltpu.SemaphoreType.DMA((6,))],
    )
    recv = to_all(sent)
    coef1, level1 = call(
        coef_kernel,
        [five, level],
        slot_row,
        coarse_face.reshape(2 * AGG, LANES),
        coarse_sink.reshape(2 * AGG, LANES),
        coarse_kap,
        spaces=(pltpu.VMEM, *[pltpu.HBM] * 3),
        scratch=vmem(2 * AGG, 2 * AGG, AGG) + [pltpu.SemaphoreType.DMA((3,))],
        cost=beside,
    )
    fine, slots = call(
        ready_kernel,
        [((9 * BLK, LANES), F32), ((BLK, LANES), F32)],
        slot_row,
        *fine_args,
        spaces=(pltpu.VMEM, *[pltpu.HBM] * 5),
        scratch=held + [pltpu.SemaphoreType.DMA((5,))] + vmem(9 * BLK),
        out_spaces=(pltpu.HBM, pltpu.VMEM),
        cost=beside,
    )
    coef2, level2 = call(pair_kernel, [five, level], coef1, exchange(coef1, 1), cost=beside)
    (levels,) = call(
        upper_kernel,
        [((2 * LEVEL_ROWS + PARTS * AGG, LANES), F32)],
        coef2,
        *[exchange(coef2, b) for b in (2, 6, 4)],
        scratch=vmem(5 * AGG, 5 * AGG, 5 * AGG),
        cost=beside,
    )
    left1, below1, marks, own_edges = call(
        restrict_kernel,
        [two, two, ((8 + 2 * NARROW, LANES), F32), ((8, LANES), F32)],
        narrow,
        recv,
        level1,
        slots,
        spaces=(pltpu.SMEM,),
    )
    hot, edges = call(
        side_kernel,
        [((NARROW * CAP + 2 * NARROW, 2 * LANES), BF16), ((9 * 8, LANES), F32)],
        marks,
        own_edges,
    )
    left2, below2 = call(
        second_kernel, [two, two], left1, exchange(left1, 1), level2
    )
    (back,) = call(
        top_kernel,
        [units],
        left2,
        *[exchange(left2, b) for b in (2, 6, 4)],
        levels,
        level2,
        below2,
        level1,
        below1,
        hot,
    )
    recv = to_all(back)
    (out,) = call(post_kernel, [cells], narrow, fine, slots, recv, edges, spaces=(pltpu.SMEM,))
    return out.reshape(BLK, 2, LANES)


def solution(mesh):
    both = ("wide", "narrow")
    placed = (
        P(both, None, None),
        P(both, None, None),
        P(both, None, None),
        P(both, None),
        P(both, None),
        P(both),
        P(both, None, None),
        P(both, None, None),
        P(both, None),
    )
    return jax.shard_map(
        on_device,
        mesh=mesh,
        in_specs=placed,
        out_specs=P(both, None, None),
        check_vma=False,
    )
```

```python
import jax
import jax.numpy as jnp
from jax import lax
from jax.experimental import pallas as pl
from jax.experimental.pallas import tpu as pltpu
from jax.sharding import PartitionSpec as P

OMEGA = 0.8
KEEP = 1.0 - OMEGA
LANES = 128
BLK = 256
AGG = 64
NARROW = 32
CAP = 16
UNIT = 2 * CAP + 1
SIDE = 7
LABEL = LANES - CAP
F32, BF16, I32 = jnp.float32, jnp.bfloat16, jnp.int32


def iota(shape, dim):
    return lax.broadcasted_iota(I32, shape, dim)


def chain_next(v):
    ahead = pltpu.roll(v, LANES - 1, 1)
    below = pltpu.roll(ahead, v.shape[0] - 1, 0)
    return jnp.where(iota(v.shape, 1) == LANES - 1, below, ahead)


def chain_prev(v):
    behind = pltpu.roll(v, 1, 1)
    above = pltpu.roll(behind, 1, 0)
    return jnp.where(iota(v.shape, 1) == 0, above, behind)


def row_next(v):
    return pltpu.roll(v, LANES - 1, 1)


def row_prev(v):
    return pltpu.roll(v, 1, 1)


class Level:
    def __init__(self, faces, sinks, coupling, prev, nxt, left=None):
        self.prev, self.nxt = prev, nxt
        self.faces = faces
        self.left = [prev(f) for f in faces] if left is None else left
        diag = [s + l + f for s, l, f in zip(sinks, self.left, faces)]
        scale = OMEGA / (diag[0] * diag[1] - coupling * coupling)
        self.inv = [diag[1] * scale, diag[0] * scale, coupling * scale]

    def parts(self):
        return [*self.faces, *self.left, *self.inv]

    @classmethod
    def load(cls, part, prev, nxt):
        level = cls.__new__(cls)
        level.prev, level.nxt = prev, nxt
        level.faces, level.left, level.inv = part[0:2], part[2:4], part[4:7]
        return level

    def flow(self, v):
        return [self.left[f] * self.prev(v[f]) + self.faces[f] * self.nxt(v[f]) for f in (0, 1)]

    def step(self, r):
        return [
            self.inv[0] * r[0] + self.inv[2] * r[1],
            self.inv[2] * r[0] + self.inv[1] * r[1],
        ]

    def begin(self, source):
        g = self.step(source)
        w = self.step(self.flow(g))
        field = [(1.0 + KEEP) * a + b for a, b in zip(g, w)]
        return field, [(2.0 * KEEP) * a + b for a, b in zip(g, w)]

    def leftover(self, source, inner):
        return [(KEEP * KEEP) * a + b for a, b in zip(source, self.flow(inner))]

    def again(self, v, field):
        u = self.step(self.flow(v))
        d = self.step(self.flow([(2.0 * KEEP) * a + b for a, b in zip(v, u)]))
        return [(field[f] + (KEEP * KEEP) * v[f]) + d[f] for f in (0, 1)]


def store(ref, parts, at=0):
    for part in parts:
        ref[at : at + part.shape[0], :] = part
        at += part.shape[0]


def load(ref, count, rows, at=0):
    return [ref[at + k * rows : at + (k + 1) * rows, :] for k in range(count)]


def last_cell(shape):
    return (iota(shape, 0) == shape[0] - 1) & (iota(shape, 1) == LANES - 1)


def split2(x):
    hi = x.astype(BF16)
    return hi, (x - hi.astype(F32)).astype(BF16)


def select_rows(onehot, x):
    return jnp.dot(
        jnp.concatenate([onehot] * 2, axis=1),
        jnp.concatenate(split2(x), axis=0),
        preferred_element_type=F32,
    )


def as_bf16(mask):
    return jnp.where(mask, 1.0, 0.0).astype(BF16)


def planar(ref, rows):
    return [ref[pl.ds(f, rows, stride=2), :] for f in (0, 1)]


def start_copies(sources, targets, sems):
    copies = [
        pltpu.make_async_copy(a, b, sems.at[k]) for k, (a, b) in enumerate(zip(sources, targets))
    ]
    for copy in copies:
        copy.start()
    return copies


def fine_start(rhs, face, sink, kap, mask):
    live = mask[...].astype(F32)
    live_next = jnp.where(last_cell((BLK, LANES)), 0.0, chain_next(live))
    both = live * live_next
    sinks = planar(sink, BLK)
    coupling = kap[...] * jnp.sqrt(sinks[0] * sinks[1]) * live
    data = Level([f * both for f in planar(face, BLK)], sinks, coupling, chain_prev, chain_next)
    source = [r * live for r in planar(rhs, BLK)]
    return data, coupling, source, *data.begin(source)


def ready_kernel(slot_row, *refs):
    inputs, fine, slots, held, sems = refs[0:5], refs[5], refs[6], refs[7:12], refs[12]
    copies = start_copies(inputs, held, sems)
    slots[...] = jnp.transpose(jnp.broadcast_to(slot_row[0:1, :], (LANES, BLK)), (1, 0))
    for copy in copies:
        copy.wait()
    data, _, _, field, _ = fine_start(*held)
    store(fine, [*field, *data.parts()])


def pre_kernel(narrow, agg_hbm, *refs):
    inputs, out, slots, held, sems = refs[0:5], refs[5], refs[6], refs[7:13], refs[13]
    rhs, face, sink, kap, mask, agg = held
    n = narrow[0]
    for copy in start_copies((*inputs, agg_hbm), held, sems):
        copy.wait()

    label = agg[...]
    owner = label // AGG
    within = label - owner * AGG
    owned = iota((NARROW, BLK), 0) == owner
    before = as_bf16(iota((BLK, BLK), 0) < iota((BLK, BLK), 1))
    counts = jnp.dot(as_bf16(owned), before, preferred_element_type=F32)
    rank = jnp.sum(jnp.where(owned, counts, 0.0), axis=0, keepdims=True).astype(I32)
    slot = owner * CAP + rank
    put = as_bf16(iota((NARROW * CAP, BLK), 0) == slot)

    block = iota((1, BLK), 1)
    code = within + 1 + jnp.where(block == 0, 64, 0) + jnp.where(block == BLK - 1, 128, 0)
    coded = jnp.where(owned, code.astype(F32), 0.0).astype(BF16)
    at_rank = as_bf16(iota((LANES, BLK), 0) % CAP == rank)
    labels = lax.dot_general(
        coded, at_rank, (((1,), (1,)), ((), ())), preferred_element_type=F32
    )
    slots[...] = jnp.broadcast_to(slot.astype(F32), (8, BLK))

    data, coupling, source, _, inner = fine_start(rhs, face, sink, kap, mask)
    misfit = data.leftover(source, inner)
    row, lane = iota((BLK, LANES), 0), iota((BLK, LANES), 1)
    drop = ((row == BLK - 1) & (lane >= LANES - 3) & (n < NARROW - 1)) | (
        (row == 0) & (lane < 3) & (n > 0)
    )
    misfit = jnp.concatenate([jnp.where(drop, 0.0, m) for m in misfit], axis=1)

    rows = select_rows(put, misfit)
    for o in range(NARROW):
        for f in (0, 1):
            out[pl.ds(o * UNIT + f, CAP, stride=2), :] = rows[
                o * CAP : (o + 1) * CAP, f * LANES : (f + 1) * LANES
            ]

    lane1 = iota((1, LANES), 1)

    def ends(final, first):
        return jnp.where(lane1 >= LANES // 2, final, first)

    def rows_of(v):
        return ends(v[BLK - 1 : BLK, :], v[0:1, :])

    live_first = mask[0:1, :].astype(F32)
    live_final = mask[BLK - 1 : BLK, :].astype(F32)
    faces = []
    for f in (0, 1):
        open_face = face[2 * (BLK - 1) + f : 2 * (BLK - 1) + f + 1, :] * live_final
        final = jnp.where(lane1 == LANES - 1, open_face, data.faces[f][BLK - 1 : BLK, :])
        faces.append(ends(final, data.faces[f][0:1, :]))
    sinks = [
        ends(sink[2 * (BLK - 1) + f : 2 * (BLK - 1) + f + 1, :], sink[f : f + 1, :]) for f in (0, 1)
    ]
    quantities = [*map(rows_of, source), *faces, *sinks, rows_of(coupling)]
    edges = jnp.zeros((1, LANES), F32)
    for q, cells in enumerate(quantities):
        here = (lane1 >= 2 * SIDE * q) & (lane1 < 2 * SIDE * (q + 1))
        edges = jnp.where(here, pltpu.roll(cells, 2 * SIDE * q + SIDE, 1), edges)
    spare = 2 * SIDE * len(quantities)
    edges = jnp.where(lane1 == spare, pltpu.roll(live_first, spare, 1), edges)
    for f in (0, 1):
        before = pltpu.roll(faces[f], spare + 1 + f + SIDE + 1, 1)
        edges = jnp.where(lane1 == spare + 1 + f, before, edges)
    out[pl.ds(2 * CAP, NARROW, stride=UNIT), :] = jnp.where(
        iota((NARROW, LANES), 1) >= LABEL, labels, edges
    )


def interface_level(cells):
    lane = iota(cells.shape, 1)
    spare = 2 * SIDE * 7

    def moved(start, to):
        shift = (to - start) % LANES
        return cells if shift == 0 else pltpu.roll(cells, shift, 1)

    def quantity(q, fill):
        return jnp.where(lane < 2 * SIDE, moved(2 * SIDE * q, 0), fill)

    source = [quantity(0, 0.0), quantity(1, 0.0)]
    live_next = jnp.where(lane == SIDE - 1, moved(spare, SIDE - 1), 1.0)
    faces = [quantity(2, 0.0) * live_next, quantity(3, 0.0) * live_next]
    left = [
        jnp.where(lane == 0, moved(spare + 1 + f, 0), row_prev(faces[f])) for f in (0, 1)
    ]
    sinks = [quantity(4, 1.0), quantity(5, 1.0)]
    return Level(faces, sinks, quantity(6, 0.0), row_prev, row_next, left), source


PARTS = 7
REACH = (2, 0, -2)
TWICE = 4 * len(REACH)
LEVEL_ROWS = (PARTS + TWICE) * AGG


def shifted(v, cells):
    if cells == 0:
        return v
    moved = pltpu.roll(v, cells % LANES, 1)
    lane = iota(v.shape, 1)
    if cells > 0:
        return jnp.where(lane < cells, pltpu.roll(moved, 1, 0), moved)
    return jnp.where(lane >= LANES + cells, pltpu.roll(moved, v.shape[0] - 1, 0), moved)


def product(a, b):
    return [
        a[0] * b[0] + a[1] * b[2],
        a[0] * b[1] + a[1] * b[3],
        a[2] * b[0] + a[3] * b[2],
        a[2] * b[1] + a[3] * b[3],
    ]


def plus(a, b):
    return [x + y for x, y in zip(a, b)]


def apply_blocks(blocks, v):
    terms = []
    for k, cells in enumerate(REACH):
        block, at = blocks[4 * k : 4 * k + 4], [shifted(x, cells) for x in v]
        terms.append([block[2 * f] * at[0] + block[2 * f + 1] * at[1] for f in (0, 1)])
    return plus(terms[1], plus(terms[0], terms[2]))


class Coarse:
    @staticmethod
    def build(coef, out, at=0, again=True):
        part = load(coef, 5, AGG)
        level = Level(part[0:2], part[2:4], part[4], chain_prev, chain_next)
        store(out, level.parts(), at * LEVEL_ROWS)
        if not again:
            return
        (l0, l1), (r0, r1), (i0, i1, i2) = level.left, level.faces, level.inv
        from_left = [i0 * l0, i2 * l1, i2 * l0, i1 * l1]
        from_right = [i0 * r0, i2 * r1, i2 * r0, i1 * r1]
        left_before, right_before = ([chain_prev(x) for x in b] for b in (from_left, from_right))
        left_after, right_after = ([chain_next(x) for x in b] for b in (from_left, from_right))
        keep = jnp.full_like(l0, KEEP * KEEP)
        zero = jnp.zeros_like(l0)
        twice = [
            *product(from_left, left_before),
            *plus(
                [keep, zero, zero, keep],
                plus(product(from_left, right_before), product(from_right, left_after)),
            ),
            *product(from_right, right_after),
        ]
        store(out, twice, at * LEVEL_ROWS + PARTS * AGG)

    def __init__(self, ref, at=0):
        self.ref, self.at = ref, at * LEVEL_ROWS
        self.level = Level.load(load(ref, PARTS, AGG, self.at), chain_prev, chain_next)

    def begin(self, source):
        field, inner = self.level.begin(source)
        return field, self.level.leftover(source, inner)

    def again(self, v, field):
        near = self.level.step(self.level.flow(v))
        far = apply_blocks(load(self.ref, TWICE, AGG, self.at + PARTS * AGG), v)
        return [(field[f] + far[f]) + (2.0 * KEEP) * near[f] for f in (0, 1)]


def store2(ref, v):
    ref[0:AGG, :] = v[0]
    ref[AGG : 2 * AGG, :] = v[1]


def load2(ref):
    return [ref[0:AGG, :], ref[AGG : 2 * AGG, :]]


def coef_kernel(token, face_hbm, sink_hbm, kap_hbm, out, level, face, sink, kap, sems):
    for copy in start_copies((face_hbm, sink_hbm, kap_hbm), (face, sink, kap), sems):
        copy.wait()
    faces, sinks = planar(face, AGG), planar(sink, AGG)
    last = last_cell((AGG, LANES))
    for f in (0, 1):
        out[f * AGG : (f + 1) * AGG, :] = jnp.where(last, 0.0, faces[f])
        out[(2 + f) * AGG : (3 + f) * AGG, :] = sinks[f]
    out[4 * AGG : 5 * AGG, :] = kap[...] * jnp.sqrt(sinks[0] * sinks[1])
    Coarse.build(out, level)


def pair_kernel(mine, other, out, level):
    out[...] = mine[...] + other[...]
    Coarse.build(out, level)


def upper_kernel(coef2, coef2_a, coef2_b, coef2_c, levels, near, far, top):
    near[...] = coef2[...] + coef2_a[...]
    far[...] = coef2_b[...] + coef2_c[...]
    top[...] = near[...] + far[...]
    for k, ref in enumerate((near, top, far)):
        Coarse.build(ref, levels, k, ref is not far)


def restrict_kernel(narrow, recv, level1, token, leftover, below, marks, own_edges):
    n = narrow[0]
    lane = iota((NARROW, LANES), 1)
    src = iota((NARROW, LANES), 0)
    raw = recv[pl.ds(2 * CAP, NARROW, stride=UNIT), :]
    code = jnp.where(lane >= LABEL, raw, 0.0).astype(I32)
    plain = jnp.where(code > 0, (code - 1) % AGG, -1)

    from_end = lane > 2 * SIDE * 7
    for q in range(7):
        from_end = from_end | ((lane >= 2 * SIDE * q) & (lane < 2 * SIDE * q + SIDE))
    cells = jnp.where(from_end, raw, pltpu.roll(raw, NARROW - 1, 0))
    data, source = interface_level(cells)
    _, inner = data.begin(source)
    mis = [pltpu.roll(m, LANES - SIDE, 1) for m in data.leftover(source, inner)]
    mis = jnp.concatenate(mis, axis=1)
    wide_lane = iota((NARROW, 2 * LANES), 1) % LANES
    real = iota((NARROW, 2 * LANES), 0) < NARROW - 1
    after_end = jnp.where((wide_lane >= LANES - 3) & real, mis, 0.0)
    at_start = jnp.where((wide_lane < 3) & real, mis, 0.0)
    is_end = code > 128
    is_start = (code > 64) & (code <= 128)
    end_at = jnp.max(jnp.where(is_end, plain, -1), axis=1, keepdims=True)
    start_at = jnp.max(jnp.where(is_start, plain, -1), axis=1, keepdims=True)
    end_hot = jnp.where(lane == end_at, 1.0, 0.0)
    start_hot = jnp.where(lane == start_at, 1.0, 0.0)
    start_next = pltpu.roll(start_hot, NARROW - 1, 0)
    zeros = jnp.zeros((2 * NARROW, LANES), F32)
    hot = jnp.transpose(jnp.concatenate([end_hot, start_next, zeros], axis=0), (1, 0))
    edge_hot = hot[0:AGG, :].astype(BF16)
    edge_rows = jnp.concatenate(
        [after_end, at_start, jnp.zeros((2 * NARROW, 2 * LANES), F32)], axis=0
    )

    rows = []
    for t in range(NARROW // 8):
        spread = pltpu.roll(plain[8 * t : 8 * t + 8], CAP, 1, stride=CAP, stride_axis=0)
        mine = jnp.where(lane[0:8] // CAP == src[0:8], spread, 0)
        rows.append(jnp.sum(mine, axis=0, keepdims=True))
    total = select_rows(edge_hot, edge_rows)
    for half in (0, 1):
        hots, parts = [], []
        for t in (2 * half, 2 * half + 1):
            hots.append(iota((AGG, LANES), 0) == rows[t])
            for s in range(8 * t, 8 * t + 8):
                parts.append(
                    jnp.concatenate(
                        [recv[pl.ds(s * UNIT + f, CAP, stride=2), :] for f in (0, 1)], axis=1
                    )
                )
        total = total + select_rows(
            as_bf16(jnp.concatenate(hots, axis=1)), jnp.concatenate(parts, axis=0)
        )
    source_c = [total[:, 0:LANES], total[:, LANES:]]
    correction, rest = Coarse(level1).begin(source_c)
    store2(leftover, rest)
    store2(below, correction)

    for t in range(NARROW // 8):
        marks[t : t + 1, :] = rows[t].astype(F32)
    marks[8 : 8 + NARROW, :] = pltpu.roll(end_hot, 1, 0)
    marks[8 + NARROW : 8 + 2 * NARROW, :] = start_next
    own_edges[0:1, :] = jnp.sum(jnp.where(src == n - 1, cells, 0.0), axis=0, keepdims=True)
    own_edges[1:2, :] = jnp.sum(jnp.where(src == n, cells, 0.0), axis=0, keepdims=True)


def second_kernel(mine, other, level2, leftover, below):
    source = [a + b for a, b in zip(load2(mine), load2(other))]
    correction, rest = Coarse(level2).begin(source)
    store2(leftover, rest)
    store2(below, correction)


def side_kernel(marks, own_edges, hot, edges):
    lane = iota((LANES, LANES), 1)
    for t in range(NARROW // 8):
        mark = jnp.broadcast_to(marks[t : t + 1, :], (LANES, LANES))
        mark = jnp.transpose(mark, (1, 0)).astype(I32)
        once = as_bf16(mark == lane % AGG)
        last = as_bf16((mark == lane) & (lane < AGG))
        hot[t * LANES : (t + 1) * LANES, 0:LANES] = once
        hot[t * LANES : (t + 1) * LANES, LANES:] = last
    ends = marks[8 : 8 + 2 * NARROW, :]
    hot[NARROW * CAP :, 0:LANES] = (ends + pltpu.roll(ends, AGG, 1)).astype(BF16)
    hot[NARROW * CAP :, LANES:] = ends.astype(BF16)
    data, source = interface_level(own_edges[...])
    field, _ = data.begin(source)
    store(edges, [*field, *data.parts()])


def top_kernel(
    left2, left2_a, left2_b, left2_c, levels, level2, below2, level1, below1, hot, out
):
    source3 = [a + b for a, b in zip(load2(left2), load2(left2_a))]
    source3_far = [a + b for a, b in zip(load2(left2_b), load2(left2_c))]
    level3, level4, level3_far = [Coarse(levels, k) for k in range(3)]
    below3, rest = level3.begin(source3)
    _, rest_far = level3_far.begin(source3_far)
    v, _ = level4.begin(plus(rest, rest_far))
    v = level4.again(v, v)
    for level, field in (
        (level3, below3),
        (Coarse(level2), load2(below2)),
        (Coarse(level1), load2(below1)),
    ):
        v = level.again(plus(field, v), field)

    both = jnp.concatenate([v[0], v[1]], axis=1)
    both = jnp.concatenate([*split2(both), jnp.zeros((2 * AGG, 2 * LANES), BF16)], axis=0)
    rows = jnp.dot(hot[...], both, preferred_element_type=F32)
    for s in range(NARROW):
        for f in (0, 1):
            out[pl.ds(s * UNIT + f, CAP, stride=2), :] = rows[
                s * CAP : (s + 1) * CAP, f * LANES : (f + 1) * LANES
            ]
    ends = rows[NARROW * CAP :, :]
    lane = iota((NARROW, LANES), 1)
    halo = []
    for f in (0, 1):
        part = ends[:, f * LANES : (f + 1) * LANES]
        halo.append(jnp.where(lane >= LANES // 2, part[0:NARROW], part[NARROW:]))
    middle = (lane >= LANES // 4) & (lane < LANES * 3 // 4)
    out[pl.ds(2 * CAP, NARROW, stride=UNIT), :] = jnp.where(
        middle, pltpu.roll(halo[1], LANES // 2, 1), halo[0]
    )


def post_kernel(narrow, fine, slots, recv, edges, out):
    n = narrow[0]
    field = load(fine, 2, BLK)
    data = Level.load(load(fine, PARTS, BLK, 2 * BLK), chain_prev, chain_next)
    slot = slots[...].astype(I32)
    lane = iota((BLK, LANES), 1)
    lifted = None
    for half in (0, 1):
        hots, parts = [], []
        for t in (2 * half, 2 * half + 1):
            hots.append(slot == lane + t * LANES)
            for s in range(8 * t, 8 * t + 8):
                parts.append(
                    jnp.concatenate(
                        [recv[pl.ds(s * UNIT + f, CAP, stride=2), :] for f in (0, 1)], axis=1
                    )
                )
        term = select_rows(as_bf16(jnp.concatenate(hots, axis=1)), jnp.concatenate(parts, axis=0))
        lifted = term if lifted is None else lifted + term
    lifted = [lifted[:, 0:LANES], lifted[:, LANES:]]
    v = data.again([a + b for a, b in zip(field, lifted)], field)

    edge_field = load(edges, 2, 8)
    edge_data = Level.load(load(edges, PARTS, 8, 16), row_prev, row_next)
    lane1 = iota((1, LANES), 1)
    row8 = iota((8, LANES), 0)
    edge_v = []
    halo = jnp.sum(recv[pl.ds(2 * CAP, NARROW, stride=UNIT), :], axis=0, keepdims=True)
    for f in (0, 1):
        beyond = halo if f == 0 else pltpu.roll(halo, LANES // 2, 1)
        first = jnp.where(lane1 >= LANES // 2, beyond, lifted[f][0:1, :])
        final = jnp.where(lane1 >= LANES // 2, lifted[f][BLK - 1 : BLK, :], beyond)
        lift = jnp.where(row8 == 0, first, jnp.where(row8 == 1, final, 0.0))
        lift = jnp.where(iota((8, LANES), 1) < 2 * SIDE, pltpu.roll(lift, SIDE, 1), 0.0)
        edge_v.append(edge_field[f] + lift)
    edge_v = edge_data.again(edge_v, edge_field)
    for f in (0, 1):
        out[pl.ds(f, BLK, stride=2), :] = v[f]
        moved = pltpu.roll(edge_v[f], LANES - SIDE, 1)
        out[f : f + 1, :] = jnp.where((lane1 < 4) & (n > 0), moved[0:1, :], v[f][0:1, :])
        final = 2 * (BLK - 1) + f
        out[final : final + 1, :] = jnp.where(
            (lane1 >= LANES - 4) & (n < NARROW - 1), moved[1:2, :], v[f][BLK - 1 : BLK, :]
        )


def call(kernel, outs, *args, spaces=(), scratch=(), cost=None):
    spaces = (*spaces, *[pltpu.VMEM] * (len(args) - len(spaces)))
    args = [
        pltpu.with_memory_space_constraint(a, s) if s == pltpu.HBM else a
        for a, s in zip(args, spaces)
    ]
    return pl.pallas_call(
        kernel,
        out_shape=[jax.ShapeDtypeStruct(s, k) for s, k in outs],
        in_specs=[pl.BlockSpec(memory_space=space) for space in spaces],
        out_specs=[pl.BlockSpec(memory_space=pltpu.VMEM) for _ in outs],
        scratch_shapes=scratch,
        cost_estimate=cost,
        compiler_params=pltpu.CompilerParams(vmem_limit_bytes=32 * 1024 * 1024),
    )(*args)


def exchange(value, bits):
    return lax.ppermute(value, "wide", [(i, i ^ bits) for i in range(lax.axis_size("wide"))])


def to_all(units):
    shape = (NARROW * UNIT, 1, LANES)
    moved = lax.all_to_all(units.reshape(shape), "narrow", 0, 0, tiled=True)
    return moved.reshape(NARROW * UNIT, LANES)


def on_device(
    rhs, fine_face, fine_sink, fine_kap, cell_mask, block_aggregate, coarse_face, coarse_sink, coarse_kap
):
    narrow = lax.axis_index("narrow").astype(I32).reshape(1)
    cells = ((2 * BLK, LANES), F32)
    five, level, two = (5 * AGG, LANES), (LEVEL_ROWS, LANES), (2 * AGG, LANES)
    five, level, two = (five, F32), (level, F32), (two, F32)
    units = ((NARROW * UNIT, LANES), F32)
    vmem = lambda *rows: [pltpu.VMEM((r, LANES), F32) for r in rows]
    held = vmem(2 * BLK, 2 * BLK, 2 * BLK, BLK) + [pltpu.VMEM((BLK, LANES), I32)]
    beside = pl.CostEstimate(flops=0, bytes_accessed=4 * 1024 * 1024, transcendentals=0)
    fine_args = (
        rhs.reshape(2 * BLK, LANES),
        fine_face.reshape(2 * BLK, LANES),
        fine_sink.reshape(2 * BLK, LANES),
        fine_kap,
        cell_mask,
    )
    sent, slot_row = call(
        pre_kernel,
        [units, ((8, BLK), F32)],
        narrow,
        block_aggregate.reshape(1, BLK),
        *fine_args,
        spaces=(pltpu.SMEM, *[pltpu.HBM] * 6),
        scratch=held + [pltpu.VMEM((1, BLK), I32), pltpu.SemaphoreType.DMA((6,))],
    )
    recv = to_all(sent)
    coef1, level1 = call(
        coef_kernel,
        [five, level],
        slot_row,
        coarse_face.reshape(2 * AGG, LANES),
        coarse_sink.reshape(2 * AGG, LANES),
        coarse_kap,
        spaces=(pltpu.VMEM, *[pltpu.HBM] * 3),
        scratch=vmem(2 * AGG, 2 * AGG, AGG) + [pltpu.SemaphoreType.DMA((3,))],
        cost=beside,
    )
    fine, slots = call(
        ready_kernel,
        [((9 * BLK, LANES), F32), ((BLK, LANES), F32)],
        slot_row,
        *fine_args,
        spaces=(pltpu.VMEM, *[pltpu.HBM] * 5),
        scratch=held + [pltpu.SemaphoreType.DMA((5,))],
        cost=beside,
    )
    coef2, level2 = call(pair_kernel, [five, level], coef1, exchange(coef1, 1), cost=beside)
    (levels,) = call(
        upper_kernel,
        [((2 * LEVEL_ROWS + PARTS * AGG, LANES), F32)],
        coef2,
        *[exchange(coef2, b) for b in (2, 6, 4)],
        scratch=vmem(5 * AGG, 5 * AGG, 5 * AGG),
        cost=beside,
    )
    left1, below1, marks, own_edges = call(
        restrict_kernel,
        [two, two, ((8 + 2 * NARROW, LANES), F32), ((8, LANES), F32)],
        narrow,
        recv,
        level1,
        fine,
        spaces=(pltpu.SMEM,),
    )
    hot, edges = call(
        side_kernel,
        [((NARROW * CAP + 2 * NARROW, 2 * LANES), BF16), ((9 * 8, LANES), F32)],
        marks,
        own_edges,
    )
    left2, below2 = call(
        second_kernel, [two, two], left1, exchange(left1, 1), level2
    )
    (back,) = call(
        top_kernel,
        [units],
        left2,
        *[exchange(left2, b) for b in (2, 6, 4)],
        levels,
        level2,
        below2,
        level1,
        below1,
        hot,
    )
    recv = to_all(back)
    (out,) = call(post_kernel, [cells], narrow, fine, slots, recv, edges, spaces=(pltpu.SMEM,))
    return out.reshape(BLK, 2, LANES)


def solution(mesh):
    both = ("wide", "narrow")
    placed = (
        P(both, None, None),
        P(both, None, None),
        P(both, None, None),
        P(both, None),
        P(both, None),
        P(both),
        P(both, None, None),
        P(both, None, None),
        P(both, None),
    )
    return jax.shard_map(
        on_device,
        mesh=mesh,
        in_specs=placed,
        out_specs=P(both, None, None),
        check_vma=False,
    )
```
